32 devices in a mesh: dp: 8 (over y, x, core), tp: 4 (over z).
Axes of the slice: x: 2, y: 2, z: 4, core: 2. Of those that a mesh axis runs over, the one named last changes fastest.
Arguments:
- tokens: bfloat16 [32768, 1024], P(('dp', 'tp')), may hold values from -6 to 6
- segment_ids: int32 [64, 512], P(('dp', 'tp')), may hold values from -1 to 7, as said below
- w_query: bfloat16 [1024, 1024], P(('dp', 'tp')), may hold values from -0.1875 to 0.1875
- w_key: bfloat16 [1024, 1024], P(('dp', 'tp')), may hold values from -0.1875 to 0.1875
- w_value: bfloat16 [1024, 1024], P(('dp', 'tp')), may hold values from -0.1875 to 0.1875
- w_output: bfloat16 [1024, 1024], P(('dp', 'tp')), may hold values from -1.5 to 1.5
- bias_query: float32 [1024], replicated, may hold values from -3 to 3
- bias_value: float32 [1024], replicated, may hold values from -3 to 3
- bias_output: float32 [1024], replicated, may hold values from -3 to 3
- gain_attn: float32 [1024], replicated, may hold values from 0.5 to 1.5
- beta_attn: float32 [1024], replicated, may hold values from -3 to 3
- w_inner: bfloat16 [1024, 4096], P(None, 'tp'), may hold values from -0.1875 to 0.1875
- bias_inner: float32 [4096], P('tp'), may hold values from -3 to 3
- w_outer: bfloat16 [4096, 1024], P('tp'), may hold values from -0.09375 to 0.09375
- bias_outer: float32 [1024], replicated, may hold values from -3 to 3
- gain_ffn: float32 [1024], replicated, may hold values from 0.5 to 1.5
- beta_ffn: float32 [1024], replicated, may hold values from -3 to 3
- cotangent: bfloat16 [32768, 1024], P(('dp', 'tp'))
Outputs:
- layer_out: bfloat16 [32768, 1024], P(('dp', 'tp'))
- tokens_grad: float32 [32768, 1024], P(('dp', 'tp'))
- grad_bias_query: float32 [1024], replicated
- grad_bias_value: float32 [1024], replicated
- grad_bias_output: float32 [1024], replicated
- grad_beta_attn: float32 [1024], replicated
- grad_bias_inner: float32 [4096], P('tp')
- grad_bias_outer: float32 [1024], replicated
- grad_beta_ffn: float32 [1024], replicated
The draws below stay inside these ranges and needn't reach their ends.
Inputs may be any that keep to these rules, and one draw needn't show every extreme that they name: `segment_ids`: in each packed row of 512 slots the filled slots come first and carry their document's number within the row, starting at 0 and never falling; a row holds at most 8 documents; empty slots form the row's tail and carry -1; between 153 and 512 slots of a row are filled. Attention only joins slots of equal value.
All inputs are finite; a program needn't handle non-finite values.
Results may differ from the reference program's by a relative error of at most 0.015.
Values may be sent and summed in bfloat16 or wider, within the bound.
No kernel may reach another device: no remote copies, remote signals or barrier semaphores. Data moves between devices by JAX's collectives and lax.ppermute only.
A program may use at most 192 MiB of HBM per device.

```python
from functools import partial
import jax
import jax.numpy as jnp
from jax import lax

D = 1024
HEADS = 16
FF = 4096
SLOTS = 512
ROWS = 64
TOKENS = 32768


def draw_segment_ids(key, part):
    key = jax.random.fold_in(key, 2)
    first_key, second_key, third_key = jax.random.split(key, 3)
    least_fill = SLOTS * 3 // 10
    spacing = max(least_fill // 8, 1)
    places = jnp.arange(SLOTS, dtype=jnp.int32)[None, :]
    row_numbers = jnp.arange(ROWS, dtype=jnp.int32)[:, None]
    chosen = jax.random.randint(third_key, (), 0, ROWS)
    starts = jax.random.randint(first_key, (ROWS, SLOTS), 0, SLOTS // 4) == 0
    forced = jnp.logical_and(places % spacing == 0, places < 8 * spacing)
    starts = jnp.where(row_numbers == chosen, forced, starts)
    starts = starts.at[:, 0].set(True)
    numbers = jnp.minimum(jnp.cumsum(starts.astype(jnp.int32), axis=1) - 1, 7)
    filled = jax.random.randint(second_key, (ROWS, 1), least_fill, SLOTS + 1)
    filled = jnp.where(row_numbers == chosen, least_fill, filled)
    return jnp.where(places < filled, numbers, -1).astype(jnp.int32)


def draw_cotangent(key, part):
    key = jax.random.fold_in(key, 5)
    first_key = jax.random.fold_in(key, 0)
    rising = 3.0 ** (jnp.arange(TOKENS, dtype=jnp.float32) / TOKENS)[:, None]
    base = jax.random.normal(first_key, (TOKENS, D), jnp.float32)
    return (base * rising).astype(jnp.bfloat16)


def shard_levels(rng, shape, pieces, low, high):
    factor_of = 1.0
    for dim, parts in pieces:
        steps = jax.random.uniform(jax.random.fold_in(jax.random.fold_in(rng, 6), dim), (parts,), jnp.float32, low / len(pieces), high / len(pieces))
        factor_of = factor_of * jnp.repeat(jnp.exp(steps), shape[dim] // parts).reshape((-1,) + (1,) * (len(shape) - 1 - dim))
    return factor_of


def scatter_about(rng, shape, deviation, bound, shards=(), kind=jnp.bfloat16):
    entries = jax.random.normal(rng, shape, jnp.float32) * deviation
    if len(shards) > 0:
        entries = shard_levels(rng, shape, shards, -0.22, 0.18) * entries
    return jnp.clip(entries, min=-bound, max=bound).astype(kind)


def setup_inputs(seed: int = 0) -> dict:
    arg_keys = jax.random.split(jax.random.key(seed), 19)
    return {
        "tokens": scatter_about(arg_keys[0], (TOKENS, D), 1.0, 6.0, ((0, 32),)),
        "segment_ids": draw_segment_ids(jax.random.fold_in(arg_keys[18], 71), 0),
        "w_query": scatter_about(arg_keys[2], (D, D), D ** -0.5, 0.1875, ((0, 32),)),
        "w_key": scatter_about(arg_keys[3], (D, D), D ** -0.5, 0.1875, ((0, 32),)),
        "w_value": scatter_about(arg_keys[4], (D, D), D ** -0.5, 0.1875, ((0, 32),)),
        "w_output": scatter_about(arg_keys[5], (D, D), (D // 64) ** -0.5, 1.5, ((0, 32),)),
        "bias_query": scatter_about(arg_keys[6], (D,), 0.5, 3.0, (), jnp.float32),
        "bias_value": scatter_about(arg_keys[7], (D,), 0.5, 3.0, (), jnp.float32),
        "bias_output": scatter_about(arg_keys[8], (D,), 0.5, 3.0, (), jnp.float32),
        "gain_attn": jnp.clip(1.0 + 0.1 * jax.random.normal(arg_keys[9], (D,), jnp.float32), 0.5, 1.5),
        "beta_attn": scatter_about(arg_keys[10], (D,), 0.5, 3.0, (), jnp.float32),
        "w_inner": scatter_about(arg_keys[11], (D, FF), D ** -0.5, 0.1875, ((1, 4),)),
        "bias_inner": scatter_about(arg_keys[12], (FF,), 0.5, 3.0, ((0, 4),), jnp.float32),
        "w_outer": scatter_about(arg_keys[13], (FF, D), FF ** -0.5, 0.09375, ((0, 4),)),
        "bias_outer": scatter_about(arg_keys[14], (D,), 0.5, 3.0, (), jnp.float32),
        "gain_ffn": jnp.clip(1.0 + 0.1 * jax.random.normal(arg_keys[15], (D,), jnp.float32), 0.5, 1.5),
        "beta_ffn": scatter_about(arg_keys[16], (D,), 0.5, 3.0, (), jnp.float32),
        "cotangent": draw_cotangent(jax.random.fold_in(arg_keys[18], 71), 0),
    }


@jax.custom_vjp
def low(v):
    return lax.optimization_barrier(v.astype(jnp.bfloat16)).astype(jnp.float32)

@jax.custom_vjp
def low_back(v):
    return v

def low_keep(v):
    return (low(v), None)

def low_pass(kept, grad):
    return (grad,)

def back_keep(v):
    return (v, None)

def back_low(kept, grad):
    return (low(grad),)
low.defvjp(low_keep, low_pass)
low_back.defvjp(back_keep, back_low)
highest_precision = lax.Precision.HIGHEST
norm_epsilon = 1e-12

def matmul_high(left, right):
    return jnp.dot(left, right, precision=highest_precision)

def round_both(value):
    return low(low_back(value))

def layer_norm(resid, gain, beta):
    centered = resid - lax.optimization_barrier(jnp.mean(resid, axis=-1, keepdims=True))
    spread = lax.optimization_barrier(jnp.mean(centered * centered, axis=-1, keepdims=True))
    return centered * lax.rsqrt(spread + norm_epsilon) * gain + beta

def exact_gelu(value):
    return jax.nn.gelu(value, approximate=False)

def block_forward(weights, segments, inputs, bias_query, bias_value, bias_output, beta_attn, bias_inner, bias_outer, beta_ffn):
    w_query, w_key, w_value, w_output, gain_attn, w_inner, w_outer, gain_ffn = weights
    count = segments.shape[0]
    slots = segments.shape[1]
    model_width = inputs.shape[1]
    head_size = model_width // HEADS
    shaped = (count, slots, HEADS, head_size)
    queries = round_both(matmul_high(inputs, w_query) + bias_query)
    key_rows = round_both(matmul_high(inputs, w_key))
    value_rows = round_both(matmul_high(inputs, w_value) + bias_value)
    scores = jnp.einsum('rqhd,rkhd->rhqk', queries.reshape(shaped), key_rows.reshape(shaped), precision=highest_precision) * head_size ** (-0.5)
    same_doc = segments[:, None, :, None] == segments[:, None, None, :]
    scores = low_back(jnp.where(same_doc, scores, -1000000000.0))
    probs = low(jax.nn.softmax(scores, axis=-1))
    mixed = jnp.einsum('rhqk,rkhd->rqhd', probs, value_rows.reshape(shaped), precision=highest_precision)
    mixed = round_both(mixed.reshape(count * slots, model_width))
    branch = low_back(matmul_high(mixed, w_output) + bias_output)
    hidden = layer_norm(inputs + branch, gain_attn, beta_attn)
    inner = low_back(matmul_high(low(hidden), w_inner) + bias_inner)
    outer = low_back(matmul_high(low(exact_gelu(inner)), w_outer) + bias_outer)
    return layer_norm(hidden + outer, gain_ffn, beta_ffn)

def reference(tokens, segment_ids, w_query, w_key, w_value, w_output, bias_query, bias_value, bias_output, gain_attn, beta_attn, w_inner, bias_inner, w_outer, bias_outer, gain_ffn, beta_ffn, cotangent):
    weights = (w_query.astype(jnp.float32), w_key.astype(jnp.float32), w_value.astype(jnp.float32), w_output.astype(jnp.float32), gain_attn, w_inner.astype(jnp.float32), w_outer.astype(jnp.float32), gain_ffn)
    biases = (bias_query, bias_value, bias_output, beta_attn, bias_inner, bias_outer, beta_ffn)
    group = 4
    inputs = tokens.astype(jnp.float32).reshape(ROWS // group, group * SLOTS, D)
    segments = segment_ids.reshape(ROWS // group, group, SLOTS)
    grads_in = cotangent.astype(jnp.float32).reshape(ROWS // group, group * SLOTS, D)

    def step(totals, block):
        inputs_block, segments_block, grad_block = block
        result, pull = jax.vjp(partial(block_forward, weights, segments_block), inputs_block, *biases)
        pulled = pull(grad_block)
        totals = tuple((total + piece for total, piece in zip(totals, pulled[1:])))
        return (totals, (result, pulled[0]))
    start = tuple((jnp.zeros_like(bias) for bias in biases))
    totals, (results, input_grads) = lax.scan(step, start, (inputs, segments, grads_in))
    return (results.reshape(TOKENS, D).astype(jnp.bfloat16), input_grads.reshape(TOKENS, D), totals[0], totals[1], totals[2], totals[3], totals[4], totals[5], totals[6])
```

```python
import functools
import math

import jax
import jax.numpy as jnp
from jax import lax
from jax.experimental import pallas as pl
from jax.experimental.pallas import tpu as pltpu
from jax.sharding import Mesh
from jax.sharding import PartitionSpec as P

HEADS = 16
F32 = jnp.float32
BF16 = jnp.bfloat16
NORM_EPSILON = 1e-12
LOG2E = math.log2(math.e)
LN2 = math.log(2.0)
VMEM_LIMIT = 56 * 1024 * 1024


def dot(left, right):
    return jnp.dot(left, right, preferred_element_type=F32)


def dot_nt(left, right):
    return lax.dot_general(left, right, (((1,), (1,)), ((), ())), preferred_element_type=F32)


def column_sum(values):
    return jnp.sum(values.astype(F32), axis=0, keepdims=True)


def normalize(resid):
    centered = resid - jnp.mean(resid, axis=-1, keepdims=True)
    spread = jnp.mean(centered * centered, axis=-1, keepdims=True)
    scale = lax.rsqrt(spread + NORM_EPSILON)
    return centered * scale, scale


def norm_back(grad, gain, normal, scale):
    weighted = grad * gain
    return scale * (
        weighted
        - jnp.mean(weighted, axis=-1, keepdims=True)
        - normal * jnp.mean(weighted * normal, axis=-1, keepdims=True)
    )


def gelu_parts(value):
    size = jnp.abs(value)
    step = 1.0 / (1.0 + (0.3275911 / math.sqrt(2.0)) * size)
    bell = jnp.exp2(value * value * (-0.5 * LOG2E))
    series = step * (
        0.5 * 0.254829592
        + step
        * (
            0.5 * -0.284496736
            + step * (0.5 * 1.421413741 + step * (0.5 * -1.453152027 + step * (0.5 * 1.061405429)))
        )
    )
    tail = series * bell
    share = jnp.where(value >= 0, 1.0 - tail, tail)
    return value * share, share + value * bell * (1.0 / math.sqrt(2.0 * math.pi))


def attend_kernel(
    head_size, seg_row, seg_col, x, wq, wk, wv, bq, bv, q_out, k_out, v_out, probs_out, mixed_out
):
    rows, slots = seg_row.shape[0], seg_row.shape[2]
    group = wq.shape[1] // head_size
    factor = head_size ** (-0.5) * LOG2E
    q_out[...] = ((dot(x[...], wq[...]) + bq[...]) * factor).astype(BF16)
    k_out[...] = dot(x[...], wk[...]).astype(BF16)
    v_out[...] = (dot(x[...], wv[...]) + bv[...]).astype(BF16)
    for row in range(rows):
        span = slice(row * slots, (row + 1) * slots)
        same_doc = seg_col[span, :] == seg_row[row]
        pieces = []
        for head in range(group):
            lanes = slice(head * head_size, (head + 1) * head_size)
            scores = dot_nt(k_out[span, lanes], q_out[span, lanes])
            scores = jnp.where(same_doc, scores, -1000000000.0)
            top = jnp.max(scores, axis=0, keepdims=True)
            powers = jnp.exp2(scores - top)
            total = jnp.sum(powers, axis=0, keepdims=True)
            probs = (powers * (1.0 / total)).astype(BF16)
            probs_out[0, row * group + head] = probs
            pieces.append(dot(v_out[span, lanes].T, probs))
        mixed_out[span, :] = jnp.concatenate(pieces, axis=0).T.astype(BF16)


def attend(tokens, segments, wq, wk, wv, bq, bv):
    count, width = tokens.shape
    rows, slots = segments.shape
    head_size = width // HEADS
    groups = 4
    lanes = width // groups
    heads = HEADS // groups
    whole = lambda shape: pl.BlockSpec(shape, lambda g: (0,) * len(shape))
    column = lambda height: pl.BlockSpec((height, lanes), lambda g: (0, g))
    return pl.pallas_call(
        functools.partial(attend_kernel, head_size),
        grid=(groups,),
        in_specs=[
            whole((rows, 1, slots)),
            whole((count, 1)),
            whole((count, width)),
            column(width),
            column(width),
            column(width),
            column(1),
            column(1),
        ],
        out_specs=[
            column(count),
            column(count),
            column(count),
            pl.BlockSpec((1, rows * heads, slots, slots), lambda g: (g, 0, 0, 0)),
            column(count),
        ],
        out_shape=[
            jax.ShapeDtypeStruct((count, width), BF16),
            jax.ShapeDtypeStruct((count, width), BF16),
            jax.ShapeDtypeStruct((count, width), BF16),
            jax.ShapeDtypeStruct((groups, rows * heads, slots, slots), BF16),
            jax.ShapeDtypeStruct((count, width), BF16),
        ],
        compiler_params=pltpu.CompilerParams(vmem_limit_bytes=VMEM_LIMIT),
        cost_estimate=pl.CostEstimate(
            flops=6 * count * width * width + 16 * count * slots * width,
            bytes_accessed=40 * 2**20,
            transcendentals=count * slots * HEADS,
        ),
        name="attend",
    )(segments.reshape(rows, 1, slots), segments.reshape(count, 1), tokens, wq, wk, wv, bq, bv)


def first_norm_kernel(x, mixed, wo, bo, normal_out, scale_out):
    resid = x[...].astype(F32) + dot(mixed[...], wo[...]) + bo[...]
    normal_out[...], scale_out[...] = normalize(resid)


def first_norm(tokens, mixed, wo, bo):
    count, width = tokens.shape
    tile = 256
    whole = lambda shape: pl.BlockSpec(shape, lambda i: (0,) * len(shape))
    rows = lambda cols: pl.BlockSpec((tile, cols), lambda i: (i, 0))
    return pl.pallas_call(
        first_norm_kernel,
        grid=(count // tile,),
        in_specs=[rows(width), rows(width), whole((width, width)), whole((1, width))],
        out_specs=[rows(width), rows(1)],
        out_shape=[
            jax.ShapeDtypeStruct((count, width), F32),
            jax.ShapeDtypeStruct((count, 1), F32),
        ],
        compiler_params=pltpu.CompilerParams(vmem_limit_bytes=VMEM_LIMIT),
        cost_estimate=pl.CostEstimate(
            flops=2 * count * width * width, bytes_accessed=10 * 2**20, transcendentals=0
        ),
        name="first_norm",
    )(tokens, mixed, wo, bo)


TILE = 256


def inner_kernel(normal, gain, beta, w_in, b_in, w_out, outer, slope_out, hidden):
    part = pl.program_id(0)

    @pl.when(part == 0)
    def _():
        hidden[...] = (normal[...] * gain[...] + beta[...]).astype(BF16)
        outer[...] = jnp.zeros_like(outer)

    for start in range(0, hidden.shape[0], TILE):
        span = slice(start, start + TILE)
        act, slope = gelu_parts(dot(hidden[span, :], w_in[...]) + b_in[...])
        slope_out[span, :] = slope.astype(BF16)
        outer[span, :] += dot(act.astype(BF16), w_out[...])


def inner_forward(normal, gain, beta, w_in, b_in, w_out):
    count, width = normal.shape
    units = w_in.shape[1]
    block = 1024
    whole = lambda shape: pl.BlockSpec(shape, lambda i: (0,) * len(shape))
    return pl.pallas_call(
        inner_kernel,
        grid=(units // block,),
        in_specs=[
            whole((count, width)),
            whole((1, width)),
            whole((1, width)),
            pl.BlockSpec((width, block), lambda i: (0, i)),
            pl.BlockSpec((1, block), lambda i: (0, i)),
            pl.BlockSpec((block, width), lambda i: (i, 0)),
        ],
        out_specs=[whole((count, width)), pl.BlockSpec((count, block), lambda i: (0, i))],
        out_shape=[
            jax.ShapeDtypeStruct((count, width), F32),
            jax.ShapeDtypeStruct((count, units), BF16),
        ],
        scratch_shapes=[pltpu.VMEM((count, width), BF16)],
        compiler_params=pltpu.CompilerParams(vmem_limit_bytes=VMEM_LIMIT),
        cost_estimate=pl.CostEstimate(
            flops=4 * count * width * units, bytes_accessed=32 * 2**20, transcendentals=0
        ),
        name="inner_forward",
    )(normal, gain, beta, w_in, b_in, w_out)


def inner_back_kernel(
    normal,
    scale,
    gain_attn,
    beta_attn,
    outer,
    b_out,
    gain_ffn,
    beta_ffn,
    cot,
    slope,
    w_in,
    w_out,
    layer_out,
    first_grad,
    branch_grad,
    sum_inner,
    sum_outer,
    sum_beta_ffn,
    sum_beta_attn,
    sum_output,
    hidden_grad,
    outer_grad,
):
    part = pl.program_id(0)
    count = normal.shape[0]

    @pl.when(part == 0)
    def _():
        sum_outer[...] = jnp.zeros_like(sum_outer)
        sum_beta_ffn[...] = jnp.zeros_like(sum_beta_ffn)
        for start in range(0, count, TILE):
            span = slice(start, start + TILE)
            hidden = normal[span, :] * gain_attn[...] + beta_attn[...]
            unit, scale_two = normalize(hidden + outer[span, :] + b_out[...])
            layer_out[span, :] = (unit * gain_ffn[...] + beta_ffn[...]).astype(BF16)
            grad = cot[span, :].astype(F32)
            sum_beta_ffn[...] += column_sum(grad)
            second = norm_back(grad, gain_ffn[...], unit, scale_two)
            hidden_grad[span, :] = second
            low = second.astype(BF16)
            outer_grad[span, :] = low
            sum_outer[...] += column_sum(low)

    total = jnp.zeros(sum_inner.shape, F32)
    for start in range(0, count, TILE):
        span = slice(start, start + TILE)
        back = dot_nt(outer_grad[span, :], w_out[...])
        inner_grad = (slope[span, :].astype(F32) * back).astype(BF16)
        total += column_sum(inner_grad)
        hidden_grad[span, :] += dot_nt(inner_grad, w_in[...])
    sum_inner[...] = total

    @pl.when(part == pl.num_programs(0) - 1)
    def _():
        sum_beta_attn[...] = jnp.zeros_like(sum_beta_attn)
        sum_output[...] = jnp.zeros_like(sum_output)
        for start in range(0, count, TILE):
            span = slice(start, start + TILE)
            grad = hidden_grad[span, :]
            sum_beta_attn[...] += column_sum(grad)
            first = norm_back(grad, gain_attn[...], normal[span, :], scale[span, :])
            first_grad[span, :] = first
            low = first.astype(BF16)
            branch_grad[span, :] = low
            sum_output[...] += column_sum(low)


def inner_backward(
    normal, scale, gain_attn, beta_attn, outer, b_out, gain_ffn, beta_ffn, cot, slope, w_in, w_out
):
    count, width = normal.shape
    units = w_in.shape[1]
    block = 1024
    once = dict(pipeline_mode=pl.Buffered(1))
    whole = lambda shape: pl.BlockSpec(shape, lambda i: (0,) * len(shape), **once)
    vector = whole((1, width))
    shaped = jax.ShapeDtypeStruct
    return pl.pallas_call(
        inner_back_kernel,
        grid=(units // block,),
        in_specs=[
            whole((count, width)),
            whole((count, 1)),
            vector,
            vector,
            whole((count, width)),
            vector,
            vector,
            vector,
            whole((count, width)),
            pl.BlockSpec((count, block), lambda i: (0, i)),
            pl.BlockSpec((width, block), lambda i: (0, i)),
            pl.BlockSpec((block, width), lambda i: (i, 0)),
        ],
        out_specs=[
            whole((count, width)),
            whole((count, width)),
            whole((count, width)),
            pl.BlockSpec((1, block), lambda i: (0, i)),
            vector,
            vector,
            vector,
            vector,
        ],
        out_shape=[
            shaped((count, width), BF16),
            shaped((count, width), F32),
            shaped((count, width), BF16),
            shaped((1, units), F32),
            shaped((1, width), F32),
            shaped((1, width), F32),
            shaped((1, width), F32),
            shaped((1, width), F32),
        ],
        scratch_shapes=[pltpu.VMEM((count, width), F32), pltpu.VMEM((count, width), BF16)],
        compiler_params=pltpu.CompilerParams(vmem_limit_bytes=VMEM_LIMIT),
        cost_estimate=pl.CostEstimate(
            flops=4 * count * width * units, bytes_accessed=46 * 2**20, transcendentals=0
        ),
        name="inner_backward",
    )(normal, scale, gain_attn, beta_attn, outer, b_out, gain_ffn, beta_ffn, cot, slope, w_in, w_out)


def attend_back_kernel(
    head_size, slots, branch, wo, q, k, v, mixed, probs_in, dq_out, dk_out, dv_out, sum_q, sum_v
):
    rows = branch.shape[0] // slots
    group = wo.shape[0] // head_size
    mixed_grad = dot_nt(branch[...], wo[...])
    low_grad = mixed_grad.astype(BF16)
    product = low_grad.astype(F32) * mixed[...].astype(F32)
    for row in range(rows):
        span = slice(row * slots, (row + 1) * slots)
        turned = product[span, :].T
        keys_turned = k[span, :].T
        queries_grad = []
        keys_grad = []
        values_grad = []
        for head in range(group):
            lanes = slice(head * head_size, (head + 1) * head_size)
            probs = probs_in[0, row * group + head]
            grad = low_grad[span, lanes]
            shift = jnp.sum(turned[lanes, :], axis=0, keepdims=True)
            reach = dot_nt(v[span, lanes], grad)
            score_grad = (probs.astype(F32) * (reach - shift)).astype(BF16)
            values_grad.append(dot(probs, grad))
            keys_grad.append(dot(score_grad, q[span, lanes]))
            queries_grad.append(dot(keys_turned[lanes, :], score_grad))
        dv_out[span, :] = jnp.concatenate(values_grad, axis=1).astype(BF16)
        dk_out[span, :] = (jnp.concatenate(keys_grad, axis=1) * LN2).astype(BF16)
        dq_out[span, :] = (jnp.concatenate(queries_grad, axis=0).T * head_size ** (-0.5)).astype(BF16)
    sum_q[...] = column_sum(dq_out[...])
    sum_v[...] = column_sum(dv_out[...])


def attend_backward(branch, wo, q, k, v, mixed, probs, slots):
    count, width = branch.shape
    groups, units = probs.shape[:2]
    lanes = width // groups
    column = lambda height: pl.BlockSpec((height, lanes), lambda g: (0, g))
    shaped = jax.ShapeDtypeStruct
    return pl.pallas_call(
        functools.partial(attend_back_kernel, width // HEADS, slots),
        grid=(groups,),
        in_specs=[
            pl.BlockSpec((count, width), lambda g: (0, 0)),
            pl.BlockSpec((lanes, width), lambda g: (g, 0)),
            column(count),
            column(count),
            column(count),
            column(count),
            pl.BlockSpec((1, units, slots, slots), lambda g: (g, 0, 0, 0)),
        ],
        out_specs=[column(count), column(count), column(count), column(1), column(1)],
        out_shape=[
            shaped((count, width), BF16),
            shaped((count, width), BF16),
            shaped((count, width), BF16),
            shaped((1, width), F32),
            shaped((1, width), F32),
        ],
        compiler_params=pltpu.CompilerParams(vmem_limit_bytes=VMEM_LIMIT),
        cost_estimate=pl.CostEstimate(
            flops=2 * count * width * width + 32 * count * slots * width,
            bytes_accessed=36 * 2**20,
            transcendentals=0,
        ),
        name="attend_backward",
    )(branch, wo, q, k, v, mixed, probs)


def tokens_grad_kernel(first, dq, dk, dv, wq, wk, wv, out):
    out[...] = (
        first[...] + dot_nt(dq[...], wq[...]) + dot_nt(dk[...], wk[...]) + dot_nt(dv[...], wv[...])
    )


def tokens_backward(first, dq, dk, dv, wq, wk, wv):
    count, width = first.shape
    tile = 256
    rows = pl.BlockSpec((tile, width), lambda i: (i, 0))
    whole = pl.BlockSpec((width, width), lambda i: (0, 0))
    return pl.pallas_call(
        tokens_grad_kernel,
        grid=(count // tile,),
        in_specs=[rows, rows, rows, rows, whole, whole, whole],
        out_specs=rows,
        out_shape=jax.ShapeDtypeStruct((count, width), F32),
        compiler_params=pltpu.CompilerParams(vmem_limit_bytes=VMEM_LIMIT),
        cost_estimate=pl.CostEstimate(
            flops=6 * count * width * width, bytes_accessed=20 * 2**20, transcendentals=0
        ),
        name="tokens_backward",
    )(first, dq, dk, dv, wq, wk, wv)


ALL = ("quad", "core", "tp")
DATA = ("quad", "core")


def gather_weights(w_query, w_key, w_value, w_output, w_inner, w_outer):
    parts = lax.axis_size(DATA)
    tp = lax.axis_size("tp")
    place = lax.axis_index(DATA)
    width = w_query.shape[1]
    attn = lax.all_gather(jnp.stack([w_query, w_key, w_value, w_output]), ALL, axis=1, tiled=True)
    step = w_inner.shape[0] // parts
    own = lax.dynamic_slice_in_dim(w_inner, place * step, step, 0)
    full_inner = lax.all_gather(own, ALL, axis=0)
    full_inner = full_inner.reshape(parts, tp, step, -1).transpose(0, 2, 1, 3).reshape(width, -1)
    step = w_outer.shape[0] // parts
    own = lax.dynamic_slice_in_dim(w_outer, place * step, step, 0)
    full_outer = lax.all_gather(own, ALL, axis=0)
    full_outer = full_outer.reshape(parts, tp, step, width).transpose(1, 0, 2, 3).reshape(-1, width)
    return attn[0], attn[1], attn[2], attn[3], full_inner, full_outer


def shards(
    tokens,
    segment_ids,
    w_query,
    w_key,
    w_value,
    w_output,
    bias_query,
    bias_value,
    bias_output,
    gain_attn,
    beta_attn,
    w_inner,
    bias_inner,
    w_outer,
    bias_outer,
    gain_ffn,
    beta_ffn,
    cotangent,
):
    slots = segment_ids.shape[1]
    line = lambda vector: vector.reshape(1, -1)
    full_query, full_key, full_value, full_output, full_inner, full_outer = gather_weights(
        w_query, w_key, w_value, w_output, w_inner, w_outer
    )
    bias_inner = lax.all_gather(bias_inner, "tp", axis=0, tiled=True)
    q, k, v, probs, mixed = attend(
        tokens, segment_ids, full_query, full_key, full_value, line(bias_query), line(bias_value)
    )
    normal, scale = first_norm(tokens, mixed, full_output, line(bias_output))
    outer, slope = inner_forward(
        normal, line(gain_attn), line(beta_attn), full_inner, line(bias_inner), full_outer
    )
    layer_out, first_grad, branch, sum_inner, sum_outer, sum_beta_ffn, sum_beta_attn, sum_output = (
        inner_backward(
            normal,
            scale,
            line(gain_attn),
            line(beta_attn),
            outer,
            line(bias_outer),
            line(gain_ffn),
            line(beta_ffn),
            cotangent,
            slope,
            full_inner,
            full_outer,
        )
    )
    dq, dk, dv, sum_q, sum_v = attend_backward(branch, full_output, q, k, v, mixed, probs, slots)
    tokens_grad = tokens_backward(first_grad, dq, dk, dv, full_query, full_key, full_value)
    totals = lax.psum(
        jnp.concatenate(
            [sum_q, sum_v, sum_output, sum_beta_attn, sum_outer, sum_beta_ffn, sum_inner], axis=1
        )[0],
        ALL,
    )
    width = tokens.shape[1]
    six = [totals[i * width : (i + 1) * width] for i in range(6)]
    units = w_inner.shape[1]
    inner_total = lax.dynamic_slice_in_dim(
        totals[6 * width :], lax.axis_index("tp") * units, units, 0
    )
    return (
        layer_out,
        tokens_grad,
        six[0],
        six[1],
        six[2],
        six[3],
        inner_total,
        six[4],
        six[5],
    )


def solution(mesh):
    dp, tp = mesh.shape["dp"], mesh.shape["tp"]
    split = Mesh(mesh.devices.reshape(dp // 2, 2, tp), ALL)
    spread = P(ALL, None)
    in_specs = (
        (spread,) * 6
        + (P(),) * 5
        + (P(None, "tp"), P("tp"), P("tp", None), P(), P(), P(), spread)
    )
    out_specs = (spread, spread, P(), P(), P(), P(), P("tp"), P(), P())
    return jax.shard_map(shards, mesh=split, in_specs=in_specs, out_specs=out_specs, check_vma=False)
```

```python
import functools
import math

import jax
import jax.numpy as jnp
from jax import lax
from jax.experimental import pallas as pl
from jax.experimental.pallas import tpu as pltpu
from jax.sharding import Mesh
from jax.sharding import PartitionSpec as P

HEADS = 16
F32 = jnp.float32
BF16 = jnp.bfloat16
NORM_EPSILON = 1e-12
LOG2E = math.log2(math.e)
LN2 = math.log(2.0)
MIB = 2**20
keep = pltpu.HBM
spill = pltpu.HBM


def dot(left, right):
    return jnp.dot(left, right, preferred_element_type=F32)


def dot_nt(left, right):
    return lax.dot_general(left, right, (((1,), (1,)), ((), ())), preferred_element_type=F32)


def column_sum(values):
    return jnp.sum(values.astype(F32), axis=0, keepdims=True)


def normalize(resid):
    centered = resid - jnp.mean(resid, axis=-1, keepdims=True)
    spread = jnp.mean(centered * centered, axis=-1, keepdims=True)
    scale = lax.rsqrt(spread + NORM_EPSILON)
    return centered * scale, scale


def norm_back(grad, gain, normal, scale):
    weighted = grad * gain
    return scale * (
        weighted
        - jnp.mean(weighted, axis=-1, keepdims=True)
        - normal * jnp.mean(weighted * normal, axis=-1, keepdims=True)
    )


def gelu_parts(value):
    size = jnp.abs(value)
    step = 1.0 / (1.0 + (0.3275911 / math.sqrt(2.0)) * size)
    bell = jnp.exp2(value * value * (-0.5 * LOG2E))
    series = step * (
        0.5 * 0.254829592
        + step
        * (
            0.5 * -0.284496736
            + step * (0.5 * 1.421413741 + step * (0.5 * -1.453152027 + step * (0.5 * 1.061405429)))
        )
    )
    tail = series * bell
    share = jnp.where(value >= 0, 1.0 - tail, tail)
    return value * share, share + value * bell * (1.0 / math.sqrt(2.0 * math.pi))


def block_copies(ids, pieces, first, column, target, sems):
    copies = []
    for piece in pieces:
        for block in range(piece.shape[0]):
            number = len(copies)
            height = piece.shape[2]
            start = pl.multiple_of(ids[number] * height, height)
            copies.append(
                pltpu.make_async_copy(
                    piece.at[
                        block, pl.ds(first, target.shape[0]), :, pl.ds(column, target.shape[2])
                    ],
                    target.at[:, pl.ds(start, height), :],
                    sems.at[number],
                )
            )
    return copies


def unit_copies(ids, pieces, part, first_unit, w_in, w_out, sems):
    copies = []
    number = 0
    for piece in pieces:
        height = piece.shape[2] // 2
        half = piece.shape[3] // 2
        columns = pl.ds(first_unit, half)
        for block in range(piece.shape[0]):
            start = pl.multiple_of(ids[number] * height + first_unit, height)
            upper = pl.multiple_of(ids[number] * (2 * height), 2 * height)
            lower = pl.multiple_of(ids[number] * (2 * height) + height, height)
            top, bottom = pl.ds(0, height), pl.ds(height, height)
            for which, source, target in (
                (0, piece.at[block, part, top, pl.ds(0, half)], w_in.at[pl.ds(upper, height), columns]),
                (0, piece.at[block, part, top, pl.ds(half, half)], w_in.at[pl.ds(lower, height), columns]),
                (1, piece.at[block, part, bottom, :], w_out.at[pl.ds(start, height), :]),
            ):
                copies.append(pltpu.make_async_copy(source, target, sems.at[which]))
            number += 1
    return copies


def attend_kernel(head_size, first_column, count_pieces, carried, ids, *refs):
    seg_row, seg_col, x, bq, bv = refs[:5]
    pieces = refs[6 : 6 + count_pieces]
    refs = refs[6 + count_pieces + carried :]
    q_out, k_out, v_out, probs_out, mixed_out, weights, token, sems = refs
    group = q_out.shape[1] // head_size
    factor = head_size ** (-0.5) * LOG2E

    @pl.when(pl.program_id(0) == 0)
    def _():
        token[...] = jnp.zeros_like(token)
        copies = block_copies(ids, pieces, 0, first_column, weights, sems)
        for copy in copies:
            copy.start()
        for copy in copies:
            copy.wait()

    q_out[...] = ((dot(x[...], weights[0]) + bq[...]) * factor).astype(BF16)
    k_out[...] = dot(x[...], weights[1]).astype(BF16)
    v_out[...] = (dot(x[...], weights[2]) + bv[...]).astype(BF16)
    same_doc = seg_col[...] == seg_row[0]
    parts = []
    for head in range(group):
        lanes = slice(head * head_size, (head + 1) * head_size)
        scores = dot_nt(k_out[:, lanes], q_out[:, lanes])
        scores = jnp.where(same_doc, scores, -1000000000.0)
        top = jnp.max(scores, axis=0, keepdims=True)
        powers = jnp.exp2(scores - top)
        total = jnp.sum(powers, axis=0, keepdims=True)
        probs = (powers * (1.0 / total)).astype(BF16)
        probs_out[0, 0, head] = probs
        parts.append(dot(v_out[:, lanes].T, probs))
    mixed_out[...] = jnp.concatenate(parts, axis=0).T.astype(BF16)


GROUPS = 4


def attend(tokens, segments, pieces, ids, bq, bv, group, first_column, token, carried):
    count, width = tokens.shape
    rows, slots = segments.shape
    head_size = width // HEADS
    lanes = width // GROUPS
    heads = HEADS // GROUPS
    block = lambda cols, at: pl.BlockSpec((slots, cols), lambda r, ids: (r, at))
    line = pl.BlockSpec((1, lanes), lambda r, ids: (0, group))
    anywhere = pl.BlockSpec(memory_space=pltpu.HBM)
    shaped = jax.ShapeDtypeStruct
    blocks = sum(piece.shape[0] for piece in pieces)
    return pl.pallas_call(
        functools.partial(attend_kernel, head_size, first_column, len(pieces), len(carried)),
        grid_spec=pltpu.PrefetchScalarGridSpec(
            num_scalar_prefetch=1,
            grid=(rows,),
            in_specs=[
                pl.BlockSpec((1, 1, slots), lambda r, ids: (r, 0, 0)),
                block(1, 0),
                block(width, 0),
                line,
                line,
            ]
            + [anywhere] * (1 + len(pieces) + len(carried)),
            out_specs=[
                block(lanes, group),
                block(lanes, group),
                block(lanes, group),
                pl.BlockSpec((1, 1, heads, slots, slots), lambda r, ids: (group, r, 0, 0, 0)),
                block(lanes, group),
                pl.BlockSpec((3, width, lanes), lambda r, ids: (0, 0, group)),
                pl.BlockSpec((8, 128), lambda r, ids: (0, 0)),
            ],
            scratch_shapes=[pltpu.SemaphoreType.DMA((blocks,))],
        ),
        out_shape=[
            spill((count, width), BF16),
            spill((count, width), BF16),
            spill((count, width), BF16),
            spill((GROUPS, rows, heads, slots, slots), BF16),
            spill((count, width), BF16),
            spill((3, width, width), BF16),
            shaped((8, 128), F32),
        ],
        input_output_aliases={7 + len(pieces) + i: i for i in range(len(carried))},
        compiler_params=pltpu.CompilerParams(vmem_limit_bytes=60 * MIB),
        cost_estimate=pl.CostEstimate(
            flops=(6 * count * width * width + 16 * count * slots * width) // GROUPS,
            bytes_accessed=40 * 2**20 // GROUPS,
            transcendentals=count * slots * HEADS // GROUPS,
        ),
        name="attend",
    )(
        ids,
        segments.reshape(rows, 1, slots),
        segments.reshape(count, 1),
        tokens,
        bq,
        bv,
        token,
        *pieces,
        *carried,
    )


TILE = 512


def layer_kernel(
    counts,
    ids,
    block_ids,
    x,
    mixed,
    cot,
    b_output,
    gain_attn,
    beta_attn,
    b_in,
    b_outer,
    gain_ffn,
    beta_ffn,
    *refs,
):
    own_in_ref, own_out_ref = refs[:2]
    refs = refs[2:]
    bundles = []
    for count in counts:
        bundles.append(refs[:count])
        refs = refs[count:]
    (
        layer_out,
        first_grad,
        branch_grad,
        wo_out,
        sum_inner,
        sums,
        wo,
        w_in,
        w_out,
        slopes,
        even,
        odd,
        total,
        low,
        normals,
        wo_sems,
        sems,
    ) = refs
    first = pl.program_id(0) == 0
    chunks, _, units = w_in.shape

    def output_copies():
        return block_copies(block_ids, bundles[0], 3, 0, wo, wo_sems)

    def chunk_copies(chunk):
        if chunk == 0:
            return [
                pltpu.make_async_copy(own_in_ref, w_in.at[0], sems.at[0, 0]),
                pltpu.make_async_copy(own_out_ref, w_out.at[0], sems.at[0, 1]),
            ]
        copies = []
        for number in range(2):
            copies += unit_copies(
                ids,
                bundles[1 + number],
                chunk - 1,
                number * (units // 2),
                w_in.at[chunk],
                w_out.at[chunk],
                sems.at[chunk],
            )
        return copies

    def arrived(chunk, which, target):
        whole = target.at[chunk]
        pltpu.make_async_copy(whole, whole, sems.at[chunk, which]).wait()

    @pl.when(first)
    def _():
        for copy in output_copies():
            copy.start()
        for chunk in range(chunks):
            for copy in chunk_copies(chunk):
                copy.start()
        sums[...] = jnp.zeros_like(sums)
        sum_inner[...] = jnp.zeros_like(sum_inner)
        for copy in output_copies():
            copy.wait()
        half = wo.shape[2]
        wo_out[:, :half] = wo[0]
        wo_out[:, half:] = wo[1]
        arrived(0, 0, w_in)

    resid = x[...].astype(F32) + dot(mixed[...], wo_out[...]) + b_output[...]
    normal, scale = normalize(resid)
    normals[...] = normal
    hidden = normal * gain_attn[...] + beta_attn[...]
    low[...] = hidden.astype(BF16)
    total[...] = hidden + b_outer[...]
    even[...] = dot(low[...], w_in[0]) + b_in[0]

    def ahead(pair, step, source, target):
        chunk = 2 * pair + step
        following = lax.rem(chunk + 1, chunks)
        target[...] = dot(low[...], w_in[following]) + b_in[following]
        act, slope = gelu_parts(source[...])
        slopes[chunk] = slope.astype(BF16)
        total[...] += dot(act.astype(BF16), w_out[chunk])

    @pl.loop(0, chunks // 2)
    def _(pair):
        @pl.when(first)
        def _():
            arrived(2 * pair, 1, w_out)
            arrived(2 * pair + 1, 0, w_in)
            arrived(2 * pair + 1, 1, w_out)

        @pl.when(jnp.logical_and(first, pair == 0))
        def _():
            arrived(2, 0, w_in)

        ahead(pair, 0, even, odd)
        ahead(pair, 1, odd, even)

    unit, scale_two = normalize(total[...])
    layer_out[...] = (unit * gain_ffn[...] + beta_ffn[...]).astype(BF16)
    grad = cot[...].astype(F32)
    second = norm_back(grad, gain_ffn[...], unit, scale_two)
    low[...] = second.astype(BF16)
    sums[3:4, :] += column_sum(grad)
    sums[2:3, :] += column_sum(low[...])
    total[...] = second
    even[...] = dot_nt(low[...], w_out[0])

    def back(pair, step, source, target):
        chunk = 2 * pair + step
        target[...] = dot_nt(low[...], w_out[lax.rem(chunk + 1, chunks)])
        inner_grad = (slopes[chunk].astype(F32) * source[...]).astype(BF16)
        sum_inner[chunk] += column_sum(inner_grad)
        total[...] += dot_nt(inner_grad, w_in[chunk])

    @pl.loop(0, chunks // 2)
    def _(pair):
        back(pair, 0, even, odd)
        back(pair, 1, odd, even)

    sums[1:2, :] += column_sum(total[...])
    grad = norm_back(total[...], gain_attn[...], normals[...], scale)
    first_grad[...] = grad
    branch = grad.astype(BF16)
    branch_grad[...] = branch
    sums[0:1, :] += column_sum(branch)


def layer_step(
    tokens,
    mixed,
    cot,
    b_output,
    gain_attn,
    beta_attn,
    b_in,
    b_outer,
    gain_ffn,
    beta_ffn,
    own_in,
    own_out,
    output_pieces,
    bundles,
    block_ids,
    ids,
):
    count, width = tokens.shape
    chunks, _, units = b_in.shape
    whole = lambda shape: pl.BlockSpec(shape, lambda i, *ids: (0,) * len(shape))
    rows = pl.BlockSpec((TILE, width), lambda i, *ids: (i, 0))
    vector = whole((1, width))
    held = pl.BlockSpec(memory_space=pltpu.HBM)
    shaped = jax.ShapeDtypeStruct
    pieces = [output_pieces, *bundles]
    blocks = [sum(piece.shape[0] for piece in group) for group in pieces]
    return pl.pallas_call(
        functools.partial(layer_kernel, [len(group) for group in pieces]),
        grid_spec=pltpu.PrefetchScalarGridSpec(
            num_scalar_prefetch=2,
            grid=(count // TILE,),
            in_specs=[
                rows,
                rows,
                rows,
                vector,
                vector,
                vector,
                whole((chunks, 1, units)),
                vector,
                vector,
                vector,
            ]
            + [held] * (2 + sum(len(group) for group in pieces)),
            out_specs=[
                rows,
                rows,
                rows,
                whole((width, width)),
                whole((chunks, 1, units)),
                whole((4, width)),
            ],
            scratch_shapes=[
                pltpu.VMEM((2, width, width // 2), BF16),
                pltpu.VMEM((chunks, width, units), BF16),
                pltpu.VMEM((chunks, units, width), BF16),
                pltpu.VMEM((chunks, TILE, units), BF16),
                pltpu.VMEM((TILE, units), F32),
                pltpu.VMEM((TILE, units), F32),
                pltpu.VMEM((TILE, width), F32),
                pltpu.VMEM((TILE, width), BF16),
                pltpu.VMEM((TILE, width), F32),
                pltpu.SemaphoreType.DMA((blocks[0],)),
                pltpu.SemaphoreType.DMA((chunks, 2)),
            ],
        ),
        out_shape=[
            spill((count, width), BF16),
            spill((count, width), F32),
            shaped((count, width), BF16),
            spill((width, width), BF16),
            shaped((chunks, 1, units), F32),
            shaped((4, width), F32),
        ],
        compiler_params=pltpu.CompilerParams(vmem_limit_bytes=60 * MIB),
        cost_estimate=pl.CostEstimate(
            flops=2 * count * width * (width + 4 * units * chunks),
            bytes_accessed=36 * 2**20,
            transcendentals=0,
        ),
        name="layer_step",
    )(
        ids,
        block_ids,
        tokens,
        mixed,
        cot,
        b_output,
        gain_attn,
        beta_attn,
        b_in,
        b_outer,
        gain_ffn,
        beta_ffn,
        own_in,
        own_out,
        *output_pieces,
        *bundles[0],
        *bundles[1],
    )


def attend_back_kernel(
    head_size, slots, branch, wo, q, k, v, mixed, probs_in, dq_out, dk_out, dv_out, sum_q, sum_v
):
    rows = branch.shape[0] // slots
    group = wo.shape[0] // head_size
    mixed_grad = dot_nt(branch[...], wo[...])
    low_grad = mixed_grad.astype(BF16)
    product = low_grad.astype(F32) * mixed[...].astype(F32)
    for row in range(rows):
        span = slice(row * slots, (row + 1) * slots)
        turned = product[span, :].T
        keys_turned = k[span, :].T
        queries_grad = []
        keys_grad = []
        values_grad = []
        for head in range(group):
            lanes = slice(head * head_size, (head + 1) * head_size)
            probs = probs_in[0, row, head]
            grad = low_grad[span, lanes]
            shift = jnp.sum(turned[lanes, :], axis=0, keepdims=True)
            reach = dot_nt(v[span, lanes], grad)
            score_grad = (probs.astype(F32) * (reach - shift)).astype(BF16)
            values_grad.append(dot(probs, grad))
            keys_grad.append(dot(score_grad, q[span, lanes]))
            queries_grad.append(dot(keys_turned[lanes, :], score_grad))
        dv_out[span, :] = jnp.concatenate(values_grad, axis=1).astype(BF16)
        dk_out[span, :] = (jnp.concatenate(keys_grad, axis=1) * LN2).astype(BF16)
        dq_out[span, :] = (jnp.concatenate(queries_grad, axis=0).T * head_size ** (-0.5)).astype(BF16)
    sum_q[...] = column_sum(dq_out[...])
    sum_v[...] = column_sum(dv_out[...])


def attend_backward(branch, wo, q, k, v, mixed, probs, slots):
    count, width = branch.shape
    groups, rows, heads = probs.shape[:3]
    lanes = width // groups
    column = lambda height: pl.BlockSpec((height, lanes), lambda g: (0, g))
    shaped = jax.ShapeDtypeStruct
    return pl.pallas_call(
        functools.partial(attend_back_kernel, width // HEADS, slots),
        grid=(groups,),
        in_specs=[
            pl.BlockSpec((count, width), lambda g: (0, 0)),
            pl.BlockSpec((lanes, width), lambda g: (g, 0)),
            column(count),
            column(count),
            column(count),
            column(count),
            pl.BlockSpec((1, rows, heads, slots, slots), lambda g: (g, 0, 0, 0, 0)),
        ],
        out_specs=[column(count), column(count), column(count), column(1), column(1)],
        out_shape=[
            keep((count, width), BF16),
            keep((count, width), BF16),
            keep((count, width), BF16),
            shaped((1, width), F32),
            shaped((1, width), F32),
        ],
        compiler_params=pltpu.CompilerParams(vmem_limit_bytes=60 * MIB),
        cost_estimate=pl.CostEstimate(
            flops=2 * count * width * width + 32 * count * slots * width,
            bytes_accessed=36 * 2**20,
            transcendentals=0,
        ),
        name="attend_backward",
    )(branch, wo, q, k, v, mixed, probs)


def tokens_grad_kernel(first, dq, dk, dv, weights, out):
    out[...] = (
        first[...]
        + dot_nt(dq[...], weights[0])
        + dot_nt(dk[...], weights[1])
        + dot_nt(dv[...], weights[2])
    )


def tokens_backward(first, dq, dk, dv, weights):
    count, width = first.shape
    tile = 256
    rows = pl.BlockSpec((tile, width), lambda i: (i, 0))
    whole = pl.BlockSpec((3, width, width), lambda i: (0, 0, 0))
    return pl.pallas_call(
        tokens_grad_kernel,
        grid=(count // tile,),
        in_specs=[rows, rows, rows, rows, whole],
        out_specs=rows,
        out_shape=jax.ShapeDtypeStruct((count, width), F32),
        compiler_params=pltpu.CompilerParams(vmem_limit_bytes=60 * MIB),
        cost_estimate=pl.CostEstimate(
            flops=6 * count * width * width, bytes_accessed=20 * 2**20, transcendentals=0
        ),
        name="tokens_backward",
    )(first, dq, dk, dv, weights)


ALL = ("quad", "core", "tp")
DATA = ("quad", "core")
BLOCKS = 32


def swap(value, axis, bit):
    size = lax.axis_size(axis)
    return lax.ppermute(value, axis, [(i, i ^ bit) for i in range(size)])


def after(value, token):
    return lax.optimization_barrier((value, token))[0]


def gate(*values):
    return lax.optimization_barrier(values)


def with_sibling(pieces):
    return list(pieces) + [swap(piece, "core", 1) for piece in pieces]


SQUARE_ORDER = ((0, 1), (0, 2), (2, 3), (1, 3))


def attention_ids():
    quad, core, layer = (lax.axis_index(name) for name in ALL)
    ids = []
    for flip in (0, 1):
        for quads, layers in zip(SQUARE_ORDER, ((0, 2), (1, 3), (0, 2), (1, 3))):
            for step in quads:
                for far in layers:
                    ids.append((((quad ^ step) * 2 + (core ^ flip)) * 4) + (layer ^ far))
    return jnp.stack(ids).astype(jnp.int32)


def inner_payloads(w_inner, bias_inner, w_outer):
    place = lax.axis_index(DATA)
    units = w_inner.shape[1] // 2
    high = bias_inner.astype(BF16)
    rest = bias_inner - high.astype(F32)
    middle = rest.astype(BF16)
    low = (rest - middle.astype(F32)).astype(BF16)
    step = w_inner.shape[0] // 16
    payloads = []
    for bundle in range(2):
        span = slice(bundle * units, (bundle + 1) * units)
        rows = lax.dynamic_slice_in_dim(w_inner, place * 2 * step, 2 * step, 0)[:, span]
        payload = [
            rows[:step],
            rows[step:],
        ]
        payload = jnp.concatenate(payload, axis=1)
        more = lax.dynamic_slice_in_dim(w_outer, bundle * units + place * step, step, 0)
        bias = jnp.concatenate([part[span].reshape(1, units) for part in (high, middle, low)])
        bias = jnp.pad(bias, ((0, 13), (0, units)))
        payloads.append(jnp.concatenate([payload, more, bias])[None])
    return payloads


def inner_rest(own, far, near):
    rest = jnp.concatenate([near[:1], far, near[1:]])
    size = rest.shape[1] - 16
    units = rest.shape[2] // 2
    bias = jnp.sum(rest[:, size : size + 3, :units].astype(F32), axis=1, keepdims=True)
    return rest[None, :, :size], bias


def inner_ids():
    quad, core = (lax.axis_index(name) for name in DATA)
    ids = []
    for flip in (0, 1):
        for quads in SQUARE_ORDER_INNER:
            for step in quads:
                ids.append((quad ^ step) * 2 + (core ^ flip))
    return jnp.stack(ids).astype(jnp.int32)


SQUARE_ORDER_INNER = ((0,), (1,), (2,), (3,))


def total_over_all(vectors, inner):
    width = vectors.shape[1]
    joined = jnp.concatenate([vectors, inner.reshape(-1, width)])
    for axis, bit in (("core", 1), ("quad", 1), ("quad", 2)):
        joined = joined + swap(joined, axis, bit)
    count = vectors.shape[0]
    held = (joined.shape[0] - count) // 4
    for bit in (2, 1):
        half = joined.shape[0] - count - held * bit
        back = swap(
            jnp.concatenate([joined[:count], joined[count + half :]]), "tp", bit
        )
        joined = joined[: count + half] + back
    return joined[:count], joined[count:]


def shards(
    tokens,
    segment_ids,
    w_query,
    w_key,
    w_value,
    w_output,
    bias_query,
    bias_value,
    bias_output,
    gain_attn,
    beta_attn,
    w_inner,
    bias_inner,
    w_outer,
    bias_outer,
    gain_ffn,
    beta_ffn,
    cotangent,
):
    slots = segment_ids.shape[1]
    width = tokens.shape[1]
    line = lambda vector: vector.reshape(1, -1)
    quads, cores, layers = (lax.axis_size(name) for name in ALL)
    tuned = (quads, cores, layers) == (4, 2, 4)
    projections = jnp.stack([w_query, w_key, w_value])
    span = width // 2
    def attend_group(group, pieces, carried, token):
        first_column = group % 2 * (width // GROUPS)
        *carried, token = attend(
            tokens,
            segment_ids,
            pieces,
            block_ids,
            line(bias_query),
            line(bias_value),
            group,
            first_column,
            token,
            carried,
        )
        return carried, token

    token = jnp.zeros((8, 128), F32)
    if tuned:
        own_in, own_out, own_bias = w_inner, w_outer, bias_inner
        block_ids = attention_ids()
        unit_ids = inner_ids()
        join = jnp.concatenate
        own = [projections[None, :, :, :span]]
        both = [w_output[:, i * span : (i + 1) * span] for i in range(2)]
        own.append(join([projections[:, :, span:], jnp.stack(both)])[None])
        units_own = inner_payloads(w_inner, bias_inner, w_outer)
        pair = join([own[0], swap(own[0], "tp", 2)])
        left = join([pair, swap(pair, "quad", 1)])
        next_far = swap(after(own[1], pair), "tp", 2)
        near = swap(pair, "tp", 1)
        right = join([near, swap(near, "quad", 2)])
        next_pair = join([own[1], next_far])
        far = swap(after(units_own[0], next_far), "tp", 2)
        next_near = swap(after(next_pair, near), "tp", 1)
        first = [left, right, swap(left, "quad", 2), swap(right, "quad", 1)]
        bundle = with_sibling(first)
        next_along = (
            swap(after(next_pair, first[2:]), "quad", 1),
            swap(after(next_near, first[2:]), "quad", 2),
        )
        carried, token = attend_group(0, bundle, [], token)
        token, far, *next_along = gate(token, far, *next_along)
        left = join([next_pair, next_along[0]])
        right = join([next_near, next_along[1]])
        second = [left, right, swap(left, "quad", 2), swap(right, "quad", 1)]
        unit_near = swap(join([units_own[0], far]), "tp", 1)
        next_far = swap(after(units_own[1], token), "tp", 2)
        carried, token = attend_group(1, bundle, carried, token)
        token, unit_near, next_far, *second = gate(token, unit_near, next_far, *second)
        next_bundle = with_sibling(second)
        rest, bias = inner_rest(units_own[0], far, unit_near)
        inner_bias = [bias]
        along_x, along_y = swap(rest, "quad", 1), swap(rest, "quad", 2)
        next_near = swap(join([units_own[1], next_far]), "tp", 1)
        carried, token = attend_group(2, next_bundle, carried, token)
        token, along_x, along_y, next_near = gate(token, along_x, along_y, next_near)
        half = rest.shape[2] // 2
        next_rest, bias = inner_rest(units_own[1], next_far, next_near)
        inner_bias.append(bias)
        by_x = swap(join([along_y[:, :, half:], next_rest], axis=2), "quad", 1)
        by_y = swap(join([along_x[:, :, :half], next_rest], axis=2), "quad", 2)
        carried, token = attend_group(3, next_bundle, carried, token)
        carried[4], by_x, by_y, rest, next_rest = gate(carried[4], by_x, by_y, rest, next_rest)
        across = join([by_y[:, :, :half], by_x[:, :, :half]], axis=2)
        next_x, next_y = by_x[:, :, half:], by_y[:, :, half:]
        next_across = (
            swap(next_x[:, :, :half], "quad", 2),
            swap(next_y[:, :, half:], "quad", 1),
        )
        inner = [with_sibling([rest, *after((along_x, along_y), by_x), across])]
        inner.append(with_sibling([next_rest, next_x, next_y, join(next_across, axis=2)]))
        bundles = [bundle, next_bundle]
    else:
        full = lax.all_gather(projections, ALL, axis=1, tiled=True)
        more = lax.all_gather(w_output, ALL, axis=0, tiled=True)
        bundles = [
            jnp.concatenate(
                [full[:, :, i * span : (i + 1) * span], more[None, :, :span], more[None, :, span:]]
            )
            for i in range(2)
        ]
        bundles = [
            [bundle.reshape(5, BLOCKS, -1, span).transpose(1, 0, 2, 3)] for bundle in bundles
        ]
        block_ids = jnp.arange(BLOCKS, dtype=jnp.int32)
        units = width // 2
        full = lax.all_gather(w_inner, "tp", axis=1, tiled=True).reshape(8, 2, -1, 4, 2, units)
        own_in = full[:, :, :, 0].reshape(width, width)
        into = full[:, :, :, 1:].transpose(4, 0, 3, 2, 1, 5).reshape(2, 8, 3, -1, width)
        full = lax.all_gather(w_outer, "tp", axis=0, tiled=True).reshape(4, 2, 8, -1, width)
        own_out = full[0].reshape(width, width)
        out = full[1:].transpose(1, 2, 0, 3, 4)
        joined = jnp.concatenate([into, out], axis=3)
        inner = [[joined[0]], [joined[1]]]
        full = lax.all_gather(bias_inner, "tp", axis=0, tiled=True).reshape(4, 1, width)
        own_bias, inner_bias = full[0, 0], [full[1:, :, :units], full[1:, :, units:]]
        unit_ids = jnp.arange(8, dtype=jnp.int32)
        carried = []
        for group in range(GROUPS):
            carried, token = attend_group(group, bundles[group // 2], carried, token)
    q, k, v, probs, mixed, full_projections = carried
    layer_out, first_grad, branch, full_output, sum_inner, sums = layer_step(
        tokens,
        mixed,
        cotangent,
        line(bias_output),
        line(gain_attn),
        line(beta_attn),
        jnp.concatenate([line(own_bias)[None], jnp.concatenate(inner_bias, axis=2)]),
        line(bias_outer),
        line(gain_ffn),
        line(beta_ffn),
        own_in,
        own_out,
        bundles[1],
        inner,
        block_ids,
        unit_ids,
    )
    dq, dk, dv, sum_q, sum_v = attend_backward(branch, full_output, q, k, v, mixed, probs, slots)
    vectors = jnp.concatenate([sum_q, sum_v, sums])
    if tuned:
        totals, inner_total = total_over_all(vectors, sum_inner)
        inner_total = inner_total[0]
    else:
        totals = lax.psum(vectors, ALL)
        inner_total = lax.psum(sum_inner.reshape(-1), ALL)
        units = w_inner.shape[1]
        inner_total = lax.dynamic_slice_in_dim(inner_total, lax.axis_index("tp") * units, units, 0)
    tokens_grad = tokens_backward(first_grad, dq, dk, dv, full_projections)
    return (
        layer_out,
        tokens_grad,
        totals[0],
        totals[1],
        totals[2],
        totals[3],
        inner_total,
        totals[4],
        totals[5],
    )


def solution(mesh):
    dp, tp = mesh.shape["dp"], mesh.shape["tp"]
    split = Mesh(mesh.devices.reshape(dp // 2, 2, tp), ALL)
    spread = P(ALL, None)
    in_specs = (
        (spread,) * 6
        + (P(),) * 5
        + (P(None, "tp"), P("tp"), P("tp", None), P(), P(), P(), spread)
    )
    out_specs = (spread, spread, P(), P(), P(), P(), P("tp"), P(), P())
    return jax.shard_map(shards, mesh=split, in_specs=in_specs, out_specs=out_specs, check_vma=False)
```

```python
import functools
import math

import jax
import jax.numpy as jnp
from jax import lax
from jax.experimental import pallas as pl
from jax.experimental.pallas import tpu as pltpu
from jax.sharding import Mesh
from jax.sharding import PartitionSpec as P

HEADS = 16
F32 = jnp.float32
BF16 = jnp.bfloat16
NORM_EPSILON = 1e-12
LOG2E = math.log2(math.e)
LN2 = math.log(2.0)
MIB = 2**20
keep = pltpu.HBM
spill = pltpu.HBM


def dot(left, right):
    return jnp.dot(left, right, preferred_element_type=F32)


def dot_nt(left, right):
    return lax.dot_general(left, right, (((1,), (1,)), ((), ())), preferred_element_type=F32)


def column_sum(values):
    return jnp.sum(values.astype(F32), axis=0, keepdims=True)


def normalize(resid):
    centered = resid - jnp.mean(resid, axis=-1, keepdims=True)
    spread = jnp.mean(centered * centered, axis=-1, keepdims=True)
    scale = lax.rsqrt(spread + NORM_EPSILON)
    return centered * scale, scale


def norm_back(grad, gain, normal, scale):
    weighted = grad * gain
    return scale * (
        weighted
        - jnp.mean(weighted, axis=-1, keepdims=True)
        - normal * jnp.mean(weighted * normal, axis=-1, keepdims=True)
    )


def gelu_parts(value):
    size = jnp.abs(value)
    step = 1.0 / (1.0 + (0.3275911 / math.sqrt(2.0)) * size)
    bell = jnp.exp2(value * value * (-0.5 * LOG2E))
    series = step * (
        0.5 * 0.254829592
        + step
        * (
            0.5 * -0.284496736
            + step * (0.5 * 1.421413741 + step * (0.5 * -1.453152027 + step * (0.5 * 1.061405429)))
        )
    )
    tail = series * bell
    share = jnp.where(value >= 0, 1.0 - tail, tail)
    return value * share, share + value * bell * (1.0 / math.sqrt(2.0 * math.pi))


def block_copies(ids, pieces, first, column, target, sems):
    copies = []
    for piece in pieces:
        for block in range(piece.shape[0]):
            number = len(copies)
            height = piece.shape[2]
            start = pl.multiple_of(ids[number] * height, height)
            copies.append(
                pltpu.make_async_copy(
                    piece.at[
                        block, pl.ds(first, target.shape[0]), :, pl.ds(column, target.shape[2])
                    ],
                    target.at[:, pl.ds(start, height), :],
                    sems.at[number],
                )
            )
    return copies


def unit_copies(ids, pieces, part, first_unit, w_in, w_out, sems):
    copies = []
    per = len(pieces) // 2
    for number, piece in enumerate(pieces):
        flip, kind = divmod(number, per)
        place = ids[flip * (per - 1) + min(kind, per - 2)]
        split = per == 5 and kind >= 3
        height = piece.shape[2] if split else piece.shape[2] // 2
        half = piece.shape[3] // 2
        columns = pl.ds(first_unit, half)
        if not split or kind == 3:
            top = pl.ds(0, height)
            for lower in range(2):
                start = pl.multiple_of(place * (2 * height) + lower * height, height)
                copies.append(
                    pltpu.make_async_copy(
                        piece.at[0, part, top, pl.ds(lower * half, half)],
                        w_in.at[pl.ds(start, height), columns],
                        sems.at[0],
                    )
                )
        if not split or kind == 4:
            start = pl.multiple_of(place * height + first_unit, height)
            copies.append(
                pltpu.make_async_copy(
                    piece.at[0, part, pl.ds(0 if split else height, height), :],
                    w_out.at[pl.ds(start, height), :],
                    sems.at[1],
                )
            )
    return copies


def attend_kernel(head_size, first_column, count_pieces, carried, ids, *refs):
    seg_row, seg_col, x, bq, bv = refs[:5]
    pieces = refs[6 : 6 + count_pieces]
    refs = refs[6 + count_pieces + carried :]
    q_out, k_out, v_out, probs_out, mixed_out, weights, token, sems = refs
    group = q_out.shape[1] // head_size
    factor = head_size ** (-0.5) * LOG2E

    @pl.when(pl.program_id(0) == 0)
    def _():
        token[...] = jnp.zeros_like(token)
        copies = block_copies(ids, pieces, 0, first_column, weights, sems)
        for copy in copies:
            copy.start()
        for copy in copies:
            copy.wait()

    q_out[...] = ((dot(x[...], weights[0]) + bq[...]) * factor).astype(BF16)
    k_out[...] = dot(x[...], weights[1]).astype(BF16)
    v_out[...] = (dot(x[...], weights[2]) + bv[...]).astype(BF16)
    same_doc = seg_col[...] == seg_row[0]
    parts = []
    lanes_of = lambda head: slice(head * head_size, (head + 1) * head_size)
    every = [dot_nt(k_out[:, lanes_of(head)], q_out[:, lanes_of(head)]) for head in range(group)]
    for head in range(group):
        scores = jnp.where(same_doc, every[head], -1000000000.0)
        top = jnp.max(scores, axis=0, keepdims=True)
        powers = jnp.exp2(scores - top)
        total = jnp.sum(powers, axis=0, keepdims=True)
        probs = (powers * (1.0 / total)).astype(BF16)
        probs_out[0, 0, head] = probs
        parts.append(dot(v_out[:, lanes_of(head)].T, probs))
    mixed_out[...] = jnp.concatenate(parts, axis=0).T.astype(BF16)


GROUPS = 4


def attend(tokens, segments, pieces, ids, bq, bv, group, first_column, token, carried):
    count, width = tokens.shape
    rows, slots = segments.shape
    head_size = width // HEADS
    lanes = width // GROUPS
    heads = HEADS // GROUPS
    block = lambda cols, at: pl.BlockSpec((slots, cols), lambda r, ids: (r, at))
    line = pl.BlockSpec((1, lanes), lambda r, ids: (0, group))
    anywhere = pl.BlockSpec(memory_space=pltpu.HBM)
    shaped = jax.ShapeDtypeStruct
    blocks = sum(piece.shape[0] for piece in pieces)
    return pl.pallas_call(
        functools.partial(attend_kernel, head_size, first_column, len(pieces), len(carried)),
        grid_spec=pltpu.PrefetchScalarGridSpec(
            num_scalar_prefetch=1,
            grid=(rows,),
            in_specs=[
                pl.BlockSpec((1, 1, slots), lambda r, ids: (r, 0, 0)),
                block(1, 0),
                block(width, 0),
                line,
                line,
            ]
            + [anywhere] * (1 + len(pieces) + len(carried)),
            out_specs=[
                block(lanes, group),
                block(lanes, group),
                block(lanes, group),
                pl.BlockSpec((1, 1, heads, slots, slots), lambda r, ids: (group, r, 0, 0, 0)),
                block(lanes, group),
                pl.BlockSpec((3, width, lanes), lambda r, ids: (0, 0, group)),
                pl.BlockSpec((8, 128), lambda r, ids: (0, 0)),
            ],
            scratch_shapes=[pltpu.SemaphoreType.DMA((blocks,))],
        ),
        out_shape=[
            spill((count, width), BF16),
            spill((count, width), BF16),
            spill((count, width), BF16),
            spill((GROUPS, rows, heads, slots, slots), BF16),
            spill((count, width), BF16),
            spill((3, width, width), BF16),
            shaped((8, 128), F32),
        ],
        input_output_aliases={7 + len(pieces) + i: i for i in range(len(carried))},
        compiler_params=pltpu.CompilerParams(vmem_limit_bytes=60 * MIB),
        cost_estimate=pl.CostEstimate(
            flops=(6 * count * width * width + 16 * count * slots * width) // GROUPS,
            bytes_accessed=40 * 2**20 // GROUPS,
            transcendentals=count * slots * HEADS // GROUPS,
        ),
        name="attend",
    )(
        ids,
        segments.reshape(rows, 1, slots),
        segments.reshape(count, 1),
        tokens,
        bq,
        bv,
        token,
        *pieces,
        *carried,
    )


TILE = 512


def layer_kernel(
    counts,
    ids,
    block_ids,
    x,
    mixed,
    cot,
    b_output,
    gain_attn,
    beta_attn,
    b_in,
    b_outer,
    gain_ffn,
    beta_ffn,
    *refs,
):
    own_in_ref, own_out_ref = refs[:2]
    refs = refs[2:]
    bundles = []
    for count in counts:
        bundles.append(refs[:count])
        refs = refs[count:]
    (
        layer_out,
        first_grad,
        branch_grad,
        wo_out,
        sum_inner,
        sums,
        wo,
        w_in,
        w_out,
        slopes,
        even,
        odd,
        total,
        low,
        normals,
        wo_sems,
        sems,
    ) = refs
    first = pl.program_id(0) == 0
    chunks, _, units = w_in.shape

    def output_copies():
        return block_copies(block_ids, bundles[0], 3, 0, wo, wo_sems)

    def chunk_copies(chunk):
        if chunk == 0:
            return [
                pltpu.make_async_copy(own_in_ref, w_in.at[0], sems.at[0, 0]),
                pltpu.make_async_copy(own_out_ref, w_out.at[0], sems.at[0, 1]),
            ]
        copies = []
        for number in range(2):
            copies += unit_copies(
                ids,
                bundles[1 + number],
                chunk - 1,
                number * (units // 2),
                w_in.at[chunk],
                w_out.at[chunk],
                sems.at[chunk],
            )
        return copies

    def arrived(chunk, which, target):
        whole = target.at[chunk]
        pltpu.make_async_copy(whole, whole, sems.at[chunk, which]).wait()

    @pl.when(first)
    def _():
        for copy in output_copies():
            copy.start()
        for chunk in range(chunks):
            for copy in chunk_copies(chunk):
                copy.start()
        sums[...] = jnp.zeros_like(sums)
        sum_inner[...] = jnp.zeros_like(sum_inner)
        for copy in output_copies():
            copy.wait()
        half = wo.shape[2]
        wo_out[:, :half] = wo[0]
        wo_out[:, half:] = wo[1]
        arrived(0, 0, w_in)

    resid = x[...].astype(F32) + dot(mixed[...], wo_out[...]) + b_output[...]
    normal, scale = normalize(resid)
    normals[...] = normal
    hidden = normal * gain_attn[...] + beta_attn[...]
    low[...] = hidden.astype(BF16)
    total[...] = hidden + b_outer[...]
    even[...] = dot(low[...], w_in[0]) + b_in[0]

    def ahead(pair, step, source, target):
        chunk = 2 * pair + step
        following = lax.rem(chunk + 1, chunks)
        target[...] = dot(low[...], w_in[following]) + b_in[following]
        act, slope = gelu_parts(source[...])
        slopes[chunk] = slope.astype(BF16)
        total[...] += dot(act.astype(BF16), w_out[chunk])

    @pl.loop(0, chunks // 2)
    def _(pair):
        @pl.when(first)
        def _():
            arrived(2 * pair, 1, w_out)
            arrived(2 * pair + 1, 0, w_in)
            arrived(2 * pair + 1, 1, w_out)

        @pl.when(jnp.logical_and(first, pair == 0))
        def _():
            arrived(2, 0, w_in)

        ahead(pair, 0, even, odd)
        ahead(pair, 1, odd, even)

    unit, scale_two = normalize(total[...])
    layer_out[...] = (unit * gain_ffn[...] + beta_ffn[...]).astype(BF16)
    grad = cot[...].astype(F32)
    second = norm_back(grad, gain_ffn[...], unit, scale_two)
    low[...] = second.astype(BF16)
    sums[3:4, :] += column_sum(grad)
    sums[2:3, :] += column_sum(low[...])
    total[...] = second
    even[...] = dot_nt(low[...], w_out[0])

    def back(pair, step, source, target):
        chunk = 2 * pair + step
        target[...] = dot_nt(low[...], w_out[lax.rem(chunk + 1, chunks)])
        inner_grad = (slopes[chunk].astype(F32) * source[...]).astype(BF16)
        sum_inner[chunk] += column_sum(inner_grad)
        total[...] += dot_nt(inner_grad, w_in[chunk])

    @pl.loop(0, chunks // 2)
    def _(pair):
        back(pair, 0, even, odd)
        back(pair, 1, odd, even)

    sums[1:2, :] += column_sum(total[...])
    grad = norm_back(total[...], gain_attn[...], normals[...], scale)
    first_grad[...] = grad
    branch = grad.astype(BF16)
    branch_grad[...] = branch
    sums[0:1, :] += column_sum(branch)


def layer_step(
    tokens,
    mixed,
    cot,
    b_output,
    gain_attn,
    beta_attn,
    b_in,
    b_outer,
    gain_ffn,
    beta_ffn,
    own_in,
    own_out,
    output_pieces,
    bundles,
    block_ids,
    ids,
):
    count, width = tokens.shape
    chunks, _, units = b_in.shape
    whole = lambda shape: pl.BlockSpec(shape, lambda i, *ids: (0,) * len(shape))
    rows = pl.BlockSpec((TILE, width), lambda i, *ids: (i, 0))
    vector = whole((1, width))
    held = pl.BlockSpec(memory_space=pltpu.HBM)
    shaped = jax.ShapeDtypeStruct
    pieces = [output_pieces, *bundles]
    blocks = [sum(piece.shape[0] for piece in group) for group in pieces]
    return pl.pallas_call(
        functools.partial(layer_kernel, [len(group) for group in pieces]),
        grid_spec=pltpu.PrefetchScalarGridSpec(
            num_scalar_prefetch=2,
            grid=(count // TILE,),
            in_specs=[
                rows,
                rows,
                rows,
                vector,
                vector,
                vector,
                whole((chunks, 1, units)),
                vector,
                vector,
                vector,
            ]
            + [held] * (2 + sum(len(group) for group in pieces)),
            out_specs=[
                rows,
                rows,
                rows,
                whole((width, width)),
                whole((chunks, 1, units)),
                whole((4, width)),
            ],
            scratch_shapes=[
                pltpu.VMEM((2, width, width // 2), BF16),
                pltpu.VMEM((chunks, width, units), BF16),
                pltpu.VMEM((chunks, units, width), BF16),
                pltpu.VMEM((chunks, TILE, units), BF16),
                pltpu.VMEM((TILE, units), F32),
                pltpu.VMEM((TILE, units), F32),
                pltpu.VMEM((TILE, width), F32),
                pltpu.VMEM((TILE, width), BF16),
                pltpu.VMEM((TILE, width), F32),
                pltpu.SemaphoreType.DMA((blocks[0],)),
                pltpu.SemaphoreType.DMA((chunks, 2)),
            ],
        ),
        out_shape=[
            spill((count, width), BF16),
            spill((count, width), F32),
            shaped((count, width), BF16),
            spill((width, width), BF16),
            shaped((chunks, 1, units), F32),
            shaped((4, width), F32),
        ],
        compiler_params=pltpu.CompilerParams(vmem_limit_bytes=60 * MIB),
        cost_estimate=pl.CostEstimate(
            flops=2 * count * width * (width + 4 * units * chunks),
            bytes_accessed=36 * 2**20,
            transcendentals=0,
        ),
        name="layer_step",
    )(
        ids,
        block_ids,
        tokens,
        mixed,
        cot,
        b_output,
        gain_attn,
        beta_attn,
        b_in,
        b_outer,
        gain_ffn,
        beta_ffn,
        own_in,
        own_out,
        *output_pieces,
        *bundles[0],
        *bundles[1],
    )


def attend_back_kernel(
    head_size, slots, branch, first, wo, weights, q, k, v, mixed, probs_in, out, sum_q, sum_v, grads
):
    count = branch.shape[0]
    width = wo.shape[0]
    group = width // head_size
    low_grad = dot_nt(branch[...], wo[...]).astype(BF16)
    product = low_grad.astype(F32) * mixed[...].astype(F32)
    for row in range(count // slots):
        span = slice(row * slots, (row + 1) * slots)
        turned = product[span, :].T
        keys_turned = k[span, :].T
        queries_turned = q[span, :].T
        grad_turned = low_grad[span, :].T
        queries_grad = []
        keys_grad = []
        values_grad = []
        for head in range(group):
            lanes = slice(head * head_size, (head + 1) * head_size)
            probs = probs_in[0, row, head]
            shift = jnp.sum(turned[lanes, :], axis=0, keepdims=True)
            reach = dot_nt(v[span, lanes], low_grad[span, lanes])
            score_grad = (probs.astype(F32) * (reach - shift)).astype(BF16)
            values_grad.append(dot_nt(grad_turned[lanes, :], probs))
            keys_grad.append(dot_nt(queries_turned[lanes, :], score_grad))
            queries_grad.append(dot(keys_turned[lanes, :], score_grad))
        for place, (parts, factor) in enumerate(
            ((queries_grad, head_size ** (-0.5)), (keys_grad, LN2), (values_grad, 1.0))
        ):
            turned_back = jnp.concatenate(parts, axis=0).T * factor
            grads[span, place * width : (place + 1) * width] = turned_back.astype(BF16)
    sum_q[...] = column_sum(grads[:, :width])
    sum_v[...] = column_sum(grads[:, 2 * width :])
    joined = jnp.concatenate([weights[0], weights[1], weights[2]], axis=1)
    start = pl.program_id(0) == 0

    @pl.when(start)
    def _():
        for row in range(0, count, slots):
            span = slice(row, row + slots)
            out[span, :] = first[span, :] + dot_nt(grads[span, :], joined)

    @pl.when(jnp.logical_not(start))
    def _():
        for row in range(0, count, slots):
            span = slice(row, row + slots)
            out[span, :] += dot_nt(grads[span, :], joined)


def attend_backward(branch, first, wo, weights, q, k, v, mixed, probs, slots):
    count, width = branch.shape
    groups, rows, heads = probs.shape[:3]
    lanes = width // groups
    column = lambda height: pl.BlockSpec((height, lanes), lambda g: (0, g))
    whole = pl.BlockSpec((count, width), lambda g: (0, 0), pipeline_mode=pl.Buffered(1))
    shaped = jax.ShapeDtypeStruct
    return pl.pallas_call(
        functools.partial(attend_back_kernel, width // HEADS, slots),
        grid=(groups,),
        in_specs=[
            whole,
            whole,
            pl.BlockSpec((lanes, width), lambda g: (g, 0)),
            pl.BlockSpec((3, width, lanes), lambda g: (0, 0, g)),
            column(count),
            column(count),
            column(count),
            column(count),
            pl.BlockSpec((1, rows, heads, slots, slots), lambda g: (g, 0, 0, 0, 0)),
        ],
        out_specs=[pl.BlockSpec((count, width), lambda g: (0, 0)), column(1), column(1)],
        out_shape=[
            spill((count, width), F32),
            shaped((1, width), F32),
            shaped((1, width), F32),
        ],
        scratch_shapes=[pltpu.VMEM((count, 3 * lanes), BF16)],
        compiler_params=pltpu.CompilerParams(vmem_limit_bytes=60 * MIB),
        cost_estimate=pl.CostEstimate(
            flops=8 * count * width * width + 32 * count * slots * width,
            bytes_accessed=44 * 2**20,
            transcendentals=0,
        ),
        name="attend_backward",
    )(branch, first, wo, weights, q, k, v, mixed, probs)


ALL = ("quad", "core", "tp")
DATA = ("quad", "core")
BLOCKS = 32


def swap(value, axis, bit):
    size = lax.axis_size(axis)
    return lax.ppermute(value, axis, [(i, i ^ bit) for i in range(size)])


def after(value, token):
    return lax.optimization_barrier((value, token))[0]


def gate(*values):
    return lax.optimization_barrier(values)


def with_sibling(pieces):
    return list(pieces) + [swap(piece, "core", 1) for piece in pieces]


SQUARE_ORDER = ((0, 1), (0, 2), (2, 3), (1, 3))


def attention_ids():
    quad, core, layer = (lax.axis_index(name) for name in ALL)
    ids = []
    for flip in (0, 1):
        for quads, layers in zip(SQUARE_ORDER, ((0, 2), (1, 3), (0, 2), (1, 3))):
            for step in quads:
                for far in layers:
                    ids.append((((quad ^ step) * 2 + (core ^ flip)) * 4) + (layer ^ far))
    return jnp.stack(ids).astype(jnp.int32)


def inner_payloads(w_inner, bias_inner, w_outer):
    place = lax.axis_index(DATA)
    units = w_inner.shape[1] // 2
    high = bias_inner.astype(BF16)
    rest = bias_inner - high.astype(F32)
    middle = rest.astype(BF16)
    low = (rest - middle.astype(F32)).astype(BF16)
    step = w_inner.shape[0] // 16
    payloads = []
    for bundle in range(2):
        span = slice(bundle * units, (bundle + 1) * units)
        rows = lax.dynamic_slice_in_dim(w_inner, place * 2 * step, 2 * step, 0)[:, span]
        payload = [
            rows[:step],
            rows[step:],
        ]
        payload = jnp.concatenate(payload, axis=1)
        more = lax.dynamic_slice_in_dim(w_outer, bundle * units + place * step, step, 0)
        bias = jnp.concatenate([part[span].reshape(1, units) for part in (high, middle, low)])
        bias = jnp.pad(bias, ((0, 13), (0, units)))
        payloads.append(jnp.concatenate([payload, more, bias])[None])
    return payloads


def collect_kernel(far, near, rest, held, sems):
    size = rest.shape[2]
    sources = ((near, 0), (far, 0), (near, 1))
    inward = [
        pltpu.make_async_copy(source.at[row, pl.ds(0, size)], held.at[part], sems.at[part])
        for part, (source, row) in enumerate(sources)
    ]
    outward = [
        pltpu.make_async_copy(held.at[part], rest.at[0, part], sems.at[3 + part])
        for part in range(3)
    ]
    for copy in inward:
        copy.start()
    for part in range(3):
        inward[part].wait()
        outward[part].start()
    for copy in outward:
        copy.wait()


def inner_rest(far, near):
    size = far.shape[1] - 16
    width = far.shape[2]
    held = pl.BlockSpec(memory_space=pltpu.HBM)
    rest = pl.pallas_call(
        collect_kernel,
        in_specs=[held, held],
        out_specs=held,
        out_shape=pltpu.HBM((1, 3, size, width), BF16),
        scratch_shapes=[pltpu.VMEM((3, size, width), BF16), pltpu.SemaphoreType.DMA((6,))],
        cost_estimate=pl.CostEstimate(flops=0, bytes_accessed=12 * size * width, transcendentals=0),
        name="collect",
    )(far, near)
    parts = [part[:, size : size + 3, : width // 2] for part in (near[:1], far, near[1:])]
    bias = jnp.sum(jnp.concatenate(parts).astype(F32), axis=1, keepdims=True)
    return rest, bias


def inner_ids():
    quad, core = (lax.axis_index(name) for name in DATA)
    ids = []
    for flip in (0, 1):
        for quads in SQUARE_ORDER_INNER:
            for step in quads:
                ids.append((quad ^ step) * 2 + (core ^ flip))
    return jnp.stack(ids).astype(jnp.int32)


SQUARE_ORDER_INNER = ((0,), (1,), (2,), (3,))


def total_over_all(vectors, inner):
    width = vectors.shape[1]
    joined = jnp.concatenate([vectors, inner.reshape(-1, width)])
    for axis, bit in (("core", 1), ("quad", 1), ("quad", 2)):
        joined = joined + swap(joined, axis, bit)
    count = vectors.shape[0]
    held = (joined.shape[0] - count) // 4
    for bit in (2, 1):
        half = joined.shape[0] - count - held * bit
        back = swap(
            jnp.concatenate([joined[:count], joined[count + half :]]), "tp", bit
        )
        joined = joined[: count + half] + back
    return joined[:count], joined[count:]


def shards(
    tokens,
    segment_ids,
    w_query,
    w_key,
    w_value,
    w_output,
    bias_query,
    bias_value,
    bias_output,
    gain_attn,
    beta_attn,
    w_inner,
    bias_inner,
    w_outer,
    bias_outer,
    gain_ffn,
    beta_ffn,
    cotangent,
):
    slots = segment_ids.shape[1]
    width = tokens.shape[1]
    line = lambda vector: vector.reshape(1, -1)
    quads, cores, layers = (lax.axis_size(name) for name in ALL)
    tuned = (quads, cores, layers) == (4, 2, 4)
    projections = jnp.stack([w_query, w_key, w_value])
    span = width // 2
    def attend_group(group, pieces, carried, token):
        first_column = group % 2 * (width // GROUPS)
        *carried, token = attend(
            tokens,
            segment_ids,
            pieces,
            block_ids,
            line(bias_query),
            line(bias_value),
            group,
            first_column,
            token,
            carried,
        )
        return carried, token

    token = jnp.zeros((8, 128), F32)
    if tuned:
        own_in, own_out, own_bias = w_inner, w_outer, bias_inner
        block_ids = attention_ids()
        unit_ids = inner_ids()
        join = jnp.concatenate
        own = [projections[None, :, :, :span]]
        both = [w_output[:, i * span : (i + 1) * span] for i in range(2)]
        own.append(join([projections[:, :, span:], jnp.stack(both)])[None])
        units_own = inner_payloads(w_inner, bias_inner, w_outer)
        pair = join([own[0], swap(own[0], "tp", 2)])
        left = join([pair, swap(pair, "quad", 1)])
        next_far = swap(after(own[1], pair), "tp", 2)
        near = swap(pair, "tp", 1)
        right = join([near, swap(near, "quad", 2)])
        next_pair = join([own[1], next_far])
        far = swap(after(units_own[0], next_far), "tp", 2)
        next_near = swap(after(next_pair, near), "tp", 1)
        first = [left, right, swap(left, "quad", 2), swap(right, "quad", 1)]
        bundle = with_sibling(first)
        next_left = join([next_pair, swap(next_pair, "quad", 1)])
        next_right = join([next_near, swap(next_near, "quad", 2)])
        unit_pair = join([units_own[0], far])
        token, next_left, next_right, unit_pair = gate(token, next_left, next_right, unit_pair)
        second = [
            next_left,
            next_right,
            swap(next_left, "quad", 2),
            swap(next_right, "quad", 1),
        ]
        unit_near = swap(unit_pair, "tp", 1)
        carried, token = attend_group(0, bundle, [], token)
        token, unit_near, *second = gate(token, unit_near, *second)
        rest, bias = inner_rest(far, unit_near)
        inner_bias = [bias]
        along_x, along_y = swap(rest, "quad", 1), swap(rest, "quad", 2)
        next_far = swap(after(units_own[1], unit_near), "tp", 2)
        carried, token = attend_group(1, bundle, carried, token)
        token, along_x, along_y, next_far, *second = gate(
            token, along_x, along_y, next_far, *second
        )
        next_bundle = with_sibling(second)
        along_x, along_y, next_far, *next_bundle = gate(along_x, along_y, next_far, *next_bundle)
        half = rest.shape[2] // 2
        across = (
            swap(along_x[:, :, :half], "quad", 2),
            swap(along_y[:, :, half:], "quad", 1),
        )
        next_near = swap(join([units_own[1], next_far]), "tp", 1)
        carried, token = attend_group(2, next_bundle, carried, token)
        token, next_near, rest, along_x, along_y, *across = gate(
            token, next_near, rest, along_x, along_y, *across
        )
        next_rest, bias = inner_rest(next_far, next_near)
        inner_bias.append(bias)
        next_x, next_y = swap(next_rest, "quad", 1), swap(next_rest, "quad", 2)
        carried, token = attend_group(3, next_bundle, carried, token)
        carried[4], next_rest, next_x, next_y, rest, along_x, along_y, *across = gate(
            carried[4], next_rest, next_x, next_y, rest, along_x, along_y, *across
        )
        next_across = (
            swap(next_x[:, :, :half], "quad", 2),
            swap(next_y[:, :, half:], "quad", 1),
        )
        inner = [
            with_sibling([rest, along_x, along_y, *across]),
            with_sibling([next_rest, next_x, next_y, *next_across]),
        ]
        bundles = [bundle, next_bundle]
    else:
        full = lax.all_gather(projections, ALL, axis=1, tiled=True)
        more = lax.all_gather(w_output, ALL, axis=0, tiled=True)
        bundles = [
            jnp.concatenate(
                [full[:, :, i * span : (i + 1) * span], more[None, :, :span], more[None, :, span:]]
            )
            for i in range(2)
        ]
        bundles = [
            [bundle.reshape(5, BLOCKS, -1, span).transpose(1, 0, 2, 3)] for bundle in bundles
        ]
        block_ids = jnp.arange(BLOCKS, dtype=jnp.int32)
        units = width // 2
        full = lax.all_gather(w_inner, "tp", axis=1, tiled=True).reshape(8, 2, -1, 4, 2, units)
        own_in = full[:, :, :, 0].reshape(width, width)
        into = full[:, :, :, 1:].transpose(4, 0, 3, 2, 1, 5).reshape(2, 8, 3, -1, width)
        full = lax.all_gather(w_outer, "tp", axis=0, tiled=True).reshape(4, 2, 8, -1, width)
        own_out = full[0].reshape(width, width)
        out = full[1:].transpose(1, 2, 0, 3, 4)
        joined = jnp.concatenate([into, out], axis=3)
        inner = [[half[i : i + 1] for i in range(8)] for half in joined]
        full = lax.all_gather(bias_inner, "tp", axis=0, tiled=True).reshape(4, 1, width)
        own_bias, inner_bias = full[0, 0], [full[1:, :, :units], full[1:, :, units:]]
        unit_ids = jnp.arange(8, dtype=jnp.int32)
        carried = []
        for group in range(GROUPS):
            carried, token = attend_group(group, bundles[group // 2], carried, token)
    q, k, v, probs, mixed, full_projections = carried
    layer_out, first_grad, branch, full_output, sum_inner, sums = layer_step(
        tokens,
        mixed,
        cotangent,
        line(bias_output),
        line(gain_attn),
        line(beta_attn),
        jnp.concatenate([line(own_bias)[None], jnp.concatenate(inner_bias, axis=2)]),
        line(bias_outer),
        line(gain_ffn),
        line(beta_ffn),
        own_in,
        own_out,
        bundles[1],
        inner,
        block_ids,
        unit_ids,
    )
    tokens_grad, sum_q, sum_v = attend_backward(
        branch, first_grad, full_output, full_projections, q, k, v, mixed, probs, slots
    )
    vectors = jnp.concatenate([sum_q, sum_v, sums])
    if tuned:
        totals, inner_total = total_over_all(vectors, sum_inner)
        inner_total = inner_total[0]
    else:
        totals = lax.psum(vectors, ALL)
        inner_total = lax.psum(sum_inner.reshape(-1), ALL)
        units = w_inner.shape[1]
        inner_total = lax.dynamic_slice_in_dim(inner_total, lax.axis_index("tp") * units, units, 0)
    return (
        layer_out,
        tokens_grad,
        totals[0],
        totals[1],
        totals[2],
        totals[3],
        inner_total,
        totals[4],
        totals[5],
    )


def solution(mesh):
    dp, tp = mesh.shape["dp"], mesh.shape["tp"]
    split = Mesh(mesh.devices.reshape(dp // 2, 2, tp), ALL)
    spread = P(ALL, None)
    in_specs = (
        (spread,) * 6
        + (P(),) * 5
        + (P(None, "tp"), P("tp"), P("tp", None), P(), P(), P(), spread)
    )
    out_specs = (spread, spread, P(), P(), P(), P(), P("tp"), P(), P())
    return jax.shard_map(shards, mesh=split, in_specs=in_specs, out_specs=out_specs, check_vma=False)
```

```python
import functools
import math

import jax
import jax.numpy as jnp
from jax import lax
from jax.experimental import pallas as pl
from jax.experimental.pallas import tpu as pltpu
from jax.sharding import Mesh
from jax.sharding import PartitionSpec as P

HEADS = 16
F32 = jnp.float32
BF16 = jnp.bfloat16
NORM_EPSILON = 1e-12
LOG2E = math.log2(math.e)
LN2 = math.log(2.0)
MIB = 2**20
VMEM = 60 * MIB
keep = pltpu.HBM
spill = pltpu.HBM


def dot(left, right):
    return jnp.dot(left, right, preferred_element_type=F32)


def dot_nt(left, right):
    return lax.dot_general(left, right, (((1,), (1,)), ((), ())), preferred_element_type=F32)


def column_sum(values):
    return jnp.sum(values.astype(F32), axis=0, keepdims=True)


def normalize(resid):
    centered = resid - jnp.mean(resid, axis=-1, keepdims=True)
    spread = jnp.mean(centered * centered, axis=-1, keepdims=True)
    scale = lax.rsqrt(spread + NORM_EPSILON)
    return centered * scale, scale


def norm_back(grad, gain, normal, scale):
    weighted = grad * gain
    return scale * (
        weighted
        - jnp.mean(weighted, axis=-1, keepdims=True)
        - normal * jnp.mean(weighted * normal, axis=-1, keepdims=True)
    )


def gelu_parts(value):
    size = jnp.abs(value)
    step = 1.0 / (1.0 + (0.3275911 / math.sqrt(2.0)) * size)
    bell = jnp.exp2(value * value * (-0.5 * LOG2E))
    series = step * (
        0.5 * 0.254829592
        + step
        * (
            0.5 * -0.284496736
            + step * (0.5 * 1.421413741 + step * (0.5 * -1.453152027 + step * (0.5 * 1.061405429)))
        )
    )
    tail = series * bell
    share = jnp.where(value >= 0, 1.0 - tail, tail)
    return value * share, share + value * bell * (1.0 / math.sqrt(2.0 * math.pi))


def block_copies(ids, pieces, first, column, target, sems):
    copies = []
    for piece in pieces:
        for block in range(piece.shape[0]):
            number = len(copies)
            height = piece.shape[2]
            start = pl.multiple_of(ids[number] * height, height)
            copies.append(
                pltpu.make_async_copy(
                    piece.at[
                        block, pl.ds(first, target.shape[0]), :, pl.ds(column, target.shape[2])
                    ],
                    target.at[:, pl.ds(start, height), :],
                    sems.at[number],
                )
            )
    return copies


def unit_copies(ids, pieces, part, first_unit, w_in, w_out, sems):
    copies = []
    per = len(pieces) // 2
    for number, piece in enumerate(pieces):
        flip, kind = divmod(number, per)
        place = ids[flip * 4 + min(kind, 3)]
        split = per == 5 and kind >= 3
        height = piece.shape[2] if split else piece.shape[2] // 2
        half = piece.shape[3] // 2
        columns = pl.ds(first_unit, half)
        if not split or kind == 3:
            top = pl.ds(0, height)
            for lower in range(2):
                start = pl.multiple_of(place * (2 * height) + lower * height, height)
                copies.append(
                    pltpu.make_async_copy(
                        piece.at[0, part, top, pl.ds(lower * half, half)],
                        w_in.at[pl.ds(start, height), columns],
                        sems.at[0],
                    )
                )
        if not split or kind == 4:
            start = pl.multiple_of(place * height + first_unit, height)
            copies.append(
                pltpu.make_async_copy(
                    piece.at[0, part, pl.ds(0 if split else height, height), :],
                    w_out.at[pl.ds(start, height), :],
                    sems.at[1],
                )
            )
    return copies


def attend_kernel(head_size, first_column, count_pieces, carried, ids, *refs):
    seg_row, seg_col, x, bq, bv = refs[:5]
    pieces = refs[6 : 6 + count_pieces]
    refs = refs[6 + count_pieces + carried :]
    q_out, k_out, v_out, probs_out, mixed_out, weights, token, sems = refs
    group = q_out.shape[1] // head_size
    factor = head_size ** (-0.5) * LOG2E

    @pl.when(pl.program_id(0) == 0)
    def _():
        token[...] = jnp.zeros_like(token)
        copies = block_copies(ids, pieces, 0, first_column, weights, sems)
        for copy in copies:
            copy.start()
        for copy in copies:
            copy.wait()

    q_out[...] = ((dot(x[...], weights[0]) + bq[...]) * factor).astype(BF16)
    k_out[...] = dot(x[...], weights[1]).astype(BF16)
    v_out[...] = (dot(x[...], weights[2]) + bv[...]).astype(BF16)
    same_doc = seg_col[...] == seg_row[0]
    parts = []
    lanes_of = lambda head: slice(head * head_size, (head + 1) * head_size)
    every = [dot_nt(k_out[:, lanes_of(head)], q_out[:, lanes_of(head)]) for head in range(group)]
    for head in range(group):
        scores = jnp.where(same_doc, every[head], -1000000000.0)
        top = jnp.max(scores, axis=0, keepdims=True)
        powers = jnp.exp2(scores - top)
        total = jnp.sum(powers, axis=0, keepdims=True)
        probs = (powers * (1.0 / total)).astype(BF16)
        probs_out[0, 0, head] = probs
        parts.append(dot(v_out[:, lanes_of(head)].T, probs))
    mixed_out[...] = jnp.concatenate(parts, axis=0).T.astype(BF16)


GROUPS = 4


def attend(tokens, seg_row, seg_col, pieces, ids, bq, bv, group, first_column, token, carried):
    count, width = tokens.shape
    rows, _, slots = seg_row.shape
    head_size = width // HEADS
    lanes = width // GROUPS
    heads = HEADS // GROUPS
    block = lambda cols, at: pl.BlockSpec((slots, cols), lambda r, ids: (r, at))
    line = pl.BlockSpec((1, lanes), lambda r, ids: (0, group))
    anywhere = pl.BlockSpec(memory_space=pltpu.HBM)
    shaped = jax.ShapeDtypeStruct
    blocks = sum(piece.shape[0] for piece in pieces)
    return pl.pallas_call(
        functools.partial(attend_kernel, head_size, first_column, len(pieces), len(carried)),
        grid_spec=pltpu.PrefetchScalarGridSpec(
            num_scalar_prefetch=1,
            grid=(rows,),
            in_specs=[
                pl.BlockSpec((1, 1, slots), lambda r, ids: (r, 0, 0)),
                block(1, 0),
                block(width, 0),
                line,
                line,
            ]
            + [anywhere] * (1 + len(pieces) + len(carried)),
            out_specs=[
                block(lanes, group),
                block(lanes, group),
                block(lanes, group),
                pl.BlockSpec((1, 1, heads, slots, slots), lambda r, ids: (group, r, 0, 0, 0)),
                block(lanes, group),
                pl.BlockSpec((3, width, lanes), lambda r, ids: (0, 0, group)),
                pl.BlockSpec((8, 128), lambda r, ids: (0, 0)),
            ],
            scratch_shapes=[pltpu.SemaphoreType.DMA((blocks,))],
        ),
        out_shape=[
            spill((count, width), BF16),
            spill((count, width), BF16),
            spill((count, width), BF16),
            spill((GROUPS, rows, heads, slots, slots), BF16),
            spill((count, width), BF16),
            spill((3, width, width), BF16),
            shaped((8, 128), F32),
        ],
        input_output_aliases={7 + len(pieces) + i: i for i in range(len(carried))},
        compiler_params=pltpu.CompilerParams(vmem_limit_bytes=VMEM),
        cost_estimate=pl.CostEstimate(
            flops=(6 * count * width * width + 16 * count * slots * width) // GROUPS,
            bytes_accessed=40 * 2**20 // GROUPS,
            transcendentals=count * slots * HEADS // GROUPS,
        ),
        name="attend",
    )(
        ids,
        seg_row,
        seg_col,
        tokens,
        bq,
        bv,
        token,
        *pieces,
        *carried,
    )


TILE = 512


def first_norm_kernel(count_pieces, ids, x, mixed, bo, *refs):
    pieces = refs[:count_pieces]
    normal_out, scale_out, wo_out, wo, sems = refs[count_pieces:]

    @pl.when(pl.program_id(0) == 0)
    def _():
        copies = block_copies(ids, pieces, 3, 0, wo, sems)
        for copy in copies:
            copy.start()
        for copy in copies:
            copy.wait()
        half = wo.shape[2]
        wo_out[:, :half] = wo[0]
        wo_out[:, half:] = wo[1]

    resid = x[...].astype(F32) + dot(mixed[...], wo_out[...]) + bo[...]
    normal_out[...], scale_out[...] = normalize(resid)


def first_norm(tokens, mixed, pieces, ids, bo):
    count, width = tokens.shape
    tile = 256
    whole = lambda shape: pl.BlockSpec(shape, lambda i, ids: (0,) * len(shape))
    rows = lambda cols: pl.BlockSpec((tile, cols), lambda i, ids: (i, 0))
    held = pl.BlockSpec(memory_space=pltpu.HBM)
    blocks = sum(piece.shape[0] for piece in pieces)
    return pl.pallas_call(
        functools.partial(first_norm_kernel, len(pieces)),
        grid_spec=pltpu.PrefetchScalarGridSpec(
            num_scalar_prefetch=1,
            grid=(count // tile,),
            in_specs=[rows(width), rows(width), whole((1, width))] + [held] * len(pieces),
            out_specs=[rows(width), rows(1), whole((width, width))],
            scratch_shapes=[
                pltpu.VMEM((2, width, width // 2), BF16),
                pltpu.SemaphoreType.DMA((blocks,)),
            ],
        ),
        out_shape=[
            spill((count, width), F32),
            spill((count, 1), F32),
            spill((width, width), BF16),
        ],
        compiler_params=pltpu.CompilerParams(vmem_limit_bytes=VMEM),
        cost_estimate=pl.CostEstimate(
            flops=8 * count * width * width, bytes_accessed=16 * 2**20, transcendentals=0
        ),
        name="first_norm",
    )(ids, tokens, mixed, bo, *pieces)


def own_inner_kernel(normal, gain, beta, b_outer, w_in, b_in, w_out, total, slope_out):
    hidden = normal[...] * gain[...] + beta[...]
    act, slope = gelu_parts(dot(hidden.astype(BF16), w_in[...]) + b_in[...])
    slope_out[...] = slope.astype(BF16)
    total[...] = hidden + b_outer[...] + dot(act.astype(BF16), w_out[...])


def own_inner(normal, gain, beta, b_outer, w_in, b_in, w_out):
    count, width = normal.shape
    units = w_in.shape[1]
    tile = 256
    whole = lambda shape: pl.BlockSpec(shape, lambda i: (0,) * len(shape))
    rows = lambda cols: pl.BlockSpec((tile, cols), lambda i: (i, 0))
    vector = whole((1, width))
    return pl.pallas_call(
        own_inner_kernel,
        grid=(count // tile,),
        in_specs=[
            rows(width),
            vector,
            vector,
            vector,
            whole((width, units)),
            whole((1, units)),
            whole((units, width)),
        ],
        out_specs=[rows(width), rows(units)],
        out_shape=[spill((count, width), F32), spill((count, units), BF16)],
        compiler_params=pltpu.CompilerParams(vmem_limit_bytes=VMEM),
        cost_estimate=pl.CostEstimate(
            flops=8 * count * width * units, bytes_accessed=14 * 2**20, transcendentals=0
        ),
        name="own_inner",
    )(normal, gain, beta, b_outer, w_in, b_in, w_out)


def layer_kernel(
    counts,
    ids,
    normal,
    scale,
    before,
    slope_own,
    cot,
    gain_attn,
    beta_attn,
    b_even,
    b_odd,
    gain_ffn,
    beta_ffn,
    *refs,
):
    own_in_ref, own_out_ref = refs[:2]
    refs = refs[2:]
    bundles = []
    for count in counts:
        bundles.append(refs[:count])
        refs = refs[count:]
    (
        layer_out,
        first_grad,
        branch_grad,
        sum_inner,
        sums,
        w_in,
        w_out,
        slopes,
        even,
        odd,
        total,
        low,
        sems,
    ) = refs
    first = pl.program_id(0) == 0
    chunks, _, units = w_in.shape

    def chunk_copies(chunk):
        if chunk == 0:
            return [
                pltpu.make_async_copy(own_in_ref, w_in.at[0], sems.at[0, 0]),
                pltpu.make_async_copy(own_out_ref, w_out.at[0], sems.at[0, 1]),
            ]
        copies = []
        for number in range(2):
            copies += unit_copies(
                ids,
                bundles[number],
                chunk - 1,
                number * (units // 2),
                w_in.at[chunk],
                w_out.at[chunk],
                sems.at[chunk],
            )
        return copies

    def arrived(chunk, which, target):
        @pl.when(first)
        def _():
            whole = target.at[chunk]
            pltpu.make_async_copy(whole, whole, sems.at[chunk, which]).wait()

    @pl.when(first)
    def _():
        for chunk in (*range(1, chunks), 0):
            for copy in chunk_copies(chunk):
                copy.start()
        sums[...] = jnp.zeros_like(sums)
        sum_inner[...] = jnp.zeros_like(sum_inner)

    low[...] = (normal[...] * gain_attn[...] + beta_attn[...]).astype(BF16)
    total[...] = before[...]
    slopes[0] = slope_own[...]
    buffers = (even, odd)
    arrived(1, 0, w_in)
    biases = [jnp.concatenate([b_even[i], b_odd[i]], axis=1) for i in range(chunks - 1)]
    even[...] = dot(low[...], w_in[1]) + biases[0]
    for chunk in range(1, chunks):
        source, target = buffers[(chunk - 1) % 2], buffers[chunk % 2]
        arrived(chunk, 1, w_out)
        if chunk + 1 < chunks:
            arrived(chunk + 1, 0, w_in)
            target[...] = dot(low[...], w_in[chunk + 1]) + biases[chunk]
        act, slope = gelu_parts(source[...])
        slopes[chunk] = slope.astype(BF16)
        total[...] += dot(act.astype(BF16), w_out[chunk])
    arrived(0, 0, w_in)
    arrived(0, 1, w_out)

    unit, scale_two = normalize(total[...])
    layer_out[...] = (unit * gain_ffn[...] + beta_ffn[...]).astype(BF16)
    grad = cot[...].astype(F32)
    second = norm_back(grad, gain_ffn[...], unit, scale_two)
    low[...] = second.astype(BF16)
    sums[3:4, :] += column_sum(grad)
    sums[2:3, :] += column_sum(low[...])
    total[...] = second
    even[...] = dot_nt(low[...], w_out[0])

    def back(pair, step, source, target):
        chunk = 2 * pair + step
        target[...] = dot_nt(low[...], w_out[lax.rem(chunk + 1, chunks)])
        inner_grad = (slopes[chunk].astype(F32) * source[...]).astype(BF16)
        sum_inner[chunk] += column_sum(inner_grad)
        total[...] += dot_nt(inner_grad, w_in[chunk])

    @pl.loop(0, chunks // 2)
    def _(pair):
        back(pair, 0, even, odd)
        back(pair, 1, odd, even)

    sums[1:2, :] += column_sum(total[...])
    grad = norm_back(total[...], gain_attn[...], normal[...], scale[...])
    first_grad[...] = grad
    branch = grad.astype(BF16)
    branch_grad[...] = branch
    sums[0:1, :] += column_sum(branch)


def layer_step(
    normal,
    scale,
    before,
    slope_own,
    cot,
    gain_attn,
    beta_attn,
    b_even,
    b_odd,
    gain_ffn,
    beta_ffn,
    own_in,
    own_out,
    bundles,
    ids,
):
    count, width = normal.shape
    chunks = b_even.shape[0] + 1
    units = 2 * b_even.shape[2]
    whole = lambda shape: pl.BlockSpec(shape, lambda i, ids: (0,) * len(shape))
    rows = lambda cols: pl.BlockSpec((TILE, cols), lambda i, ids: (i, 0))
    vector = whole((1, width))
    held = pl.BlockSpec(memory_space=pltpu.HBM)
    shaped = jax.ShapeDtypeStruct
    return pl.pallas_call(
        functools.partial(layer_kernel, [len(group) for group in bundles]),
        grid_spec=pltpu.PrefetchScalarGridSpec(
            num_scalar_prefetch=1,
            grid=(count // TILE,),
            in_specs=[
                rows(width),
                rows(1),
                rows(width),
                rows(units),
                rows(width),
                vector,
                vector,
                whole(b_even.shape),
                whole(b_odd.shape),
                vector,
                vector,
            ]
            + [held] * (2 + sum(len(group) for group in bundles)),
            out_specs=[
                rows(width),
                rows(width),
                rows(width),
                whole((chunks, 1, units)),
                whole((4, width)),
            ],
            scratch_shapes=[
                pltpu.VMEM((chunks, width, units), BF16),
                pltpu.VMEM((chunks, units, width), BF16),
                pltpu.VMEM((chunks, TILE, units), BF16),
                pltpu.VMEM((TILE, units), F32),
                pltpu.VMEM((TILE, units), F32),
                pltpu.VMEM((TILE, width), F32),
                pltpu.VMEM((TILE, width), BF16),
                pltpu.SemaphoreType.DMA((chunks, 2)),
            ],
        ),
        out_shape=[
            spill((count, width), BF16),
            spill((count, width), F32),
            spill((count, width), BF16),
            shaped((chunks, 1, units), F32),
            shaped((4, width), F32),
        ],
        compiler_params=pltpu.CompilerParams(vmem_limit_bytes=VMEM),
        cost_estimate=pl.CostEstimate(
            flops=2 * count * width * (4 * units * chunks),
            bytes_accessed=36 * 2**20,
            transcendentals=0,
        ),
        name="layer_step",
    )(
        ids,
        normal,
        scale,
        before,
        slope_own,
        cot,
        gain_attn,
        beta_attn,
        b_even,
        b_odd,
        gain_ffn,
        beta_ffn,
        own_in,
        own_out,
        *bundles[0],
        *bundles[1],
    )


def attend_back_kernel(
    head_size, slots, branch, first, wo, weights, q, k, v, mixed, probs_in, out, sum_q, sum_v, grads
):
    count = branch.shape[0]
    width = wo.shape[0]
    group = width // head_size
    low_grad = dot_nt(branch[...], wo[...]).astype(BF16)
    product = low_grad.astype(F32) * mixed[...].astype(F32)
    for row in range(count // slots):
        span = slice(row * slots, (row + 1) * slots)
        turned = product[span, :].T
        keys_turned = k[span, :].T
        queries_turned = q[span, :].T
        grad_turned = low_grad[span, :].T
        queries_grad = []
        keys_grad = []
        values_grad = []
        for head in range(group):
            lanes = slice(head * head_size, (head + 1) * head_size)
            probs = probs_in[0, row, head]
            shift = jnp.sum(turned[lanes, :], axis=0, keepdims=True)
            reach = dot_nt(v[span, lanes], low_grad[span, lanes])
            score_grad = (probs.astype(F32) * (reach - shift)).astype(BF16)
            values_grad.append(dot_nt(grad_turned[lanes, :], probs))
            keys_grad.append(dot_nt(queries_turned[lanes, :], score_grad))
            queries_grad.append(dot(keys_turned[lanes, :], score_grad))
        for place, (parts, factor) in enumerate(
            ((queries_grad, head_size ** (-0.5)), (keys_grad, LN2), (values_grad, 1.0))
        ):
            turned_back = jnp.concatenate(parts, axis=0).T * factor
            grads[span, place * width : (place + 1) * width] = turned_back.astype(BF16)
    sum_q[...] = column_sum(grads[:, :width])
    sum_v[...] = column_sum(grads[:, 2 * width :])
    joined = jnp.concatenate([weights[0], weights[1], weights[2]], axis=1)
    start = pl.program_id(0) == 0

    @pl.when(start)
    def _():
        for row in range(0, count, slots):
            span = slice(row, row + slots)
            out[span, :] = first[span, :] + dot_nt(grads[span, :], joined)

    @pl.when(jnp.logical_not(start))
    def _():
        for row in range(0, count, slots):
            span = slice(row, row + slots)
            out[span, :] += dot_nt(grads[span, :], joined)


def attend_backward(branch, first, wo, weights, q, k, v, mixed, probs, slots):
    count, width = branch.shape
    groups, rows, heads = probs.shape[:3]
    lanes = width // groups
    column = lambda height: pl.BlockSpec((height, lanes), lambda g: (0, g))
    whole = pl.BlockSpec((count, width), lambda g: (0, 0), pipeline_mode=pl.Buffered(1))
    shaped = jax.ShapeDtypeStruct
    return pl.pallas_call(
        functools.partial(attend_back_kernel, width // HEADS, slots),
        grid=(groups,),
        in_specs=[
            whole,
            whole,
            pl.BlockSpec((lanes, width), lambda g: (g, 0)),
            pl.BlockSpec((3, width, lanes), lambda g: (0, 0, g)),
            column(count),
            column(count),
            column(count),
            column(count),
            pl.BlockSpec((1, rows, heads, slots, slots), lambda g: (g, 0, 0, 0, 0)),
        ],
        out_specs=[pl.BlockSpec((count, width), lambda g: (0, 0)), column(1), column(1)],
        out_shape=[
            spill((count, width), F32),
            shaped((1, width), F32),
            shaped((1, width), F32),
        ],
        scratch_shapes=[pltpu.VMEM((count, 3 * lanes), BF16)],
        compiler_params=pltpu.CompilerParams(vmem_limit_bytes=VMEM),
        cost_estimate=pl.CostEstimate(
            flops=8 * count * width * width + 32 * count * slots * width,
            bytes_accessed=44 * 2**20,
            transcendentals=0,
        ),
        name="attend_backward",
    )(branch, first, wo, weights, q, k, v, mixed, probs)


ALL = ("quad", "core", "tp")
DATA = ("quad", "core")
BLOCKS = 32


def swap(value, axis, bit):
    size = lax.axis_size(axis)
    return lax.ppermute(value, axis, [(i, i ^ bit) for i in range(size)])


def after(value, token):
    return lax.optimization_barrier((value, token))[0]


def gate(*values):
    return lax.optimization_barrier(values)


def with_sibling(pieces):
    return list(pieces) + [swap(piece, "core", 1) for piece in pieces]


SQUARE_ORDER = ((0, 1), (0, 2), (2, 3), (1, 3))


def attention_ids():
    quad, core, layer = (lax.axis_index(name) for name in ALL)
    ids = []
    for flip in (0, 1):
        for quads, layers in zip(SQUARE_ORDER, ((0, 2), (1, 3), (0, 2), (1, 3))):
            for step in quads:
                for far in layers:
                    ids.append((((quad ^ step) * 2 + (core ^ flip)) * 4) + (layer ^ far))
    return jnp.stack(ids).astype(jnp.int32)


def inner_payloads(w_inner, bias_inner, w_outer):
    place = lax.axis_index(DATA)
    units = w_inner.shape[1] // 2
    high = bias_inner.astype(BF16)
    rest = bias_inner - high.astype(F32)
    middle = rest.astype(BF16)
    low = (rest - middle.astype(F32)).astype(BF16)
    step = w_inner.shape[0] // 16
    payloads = []
    for bundle in range(2):
        span = slice(bundle * units, (bundle + 1) * units)
        rows = lax.dynamic_slice_in_dim(w_inner, place * 2 * step, 2 * step, 0)[:, span]
        payload = [
            rows[:step],
            rows[step:],
        ]
        payload = jnp.concatenate(payload, axis=1)
        more = lax.dynamic_slice_in_dim(w_outer, bundle * units + place * step, step, 0)
        bias = jnp.concatenate([part[span].reshape(1, units) for part in (high, middle, low)])
        bias = jnp.pad(bias, ((0, 13), (0, units)))
        payloads.append(jnp.concatenate([payload, more, bias])[None])
    return payloads


def collect_kernel(far, near, rest, bias, held, rows, sems):
    size = rest.shape[2]
    units = bias.shape[2]
    sources = ((near, 0), (far, 0), (near, 1))
    inward = [
        pltpu.make_async_copy(source.at[row, pl.ds(0, size)], held.at[part], sems.at[part])
        for part, (source, row) in enumerate(sources)
    ]
    outward = [
        pltpu.make_async_copy(held.at[part], rest.at[0, part], sems.at[3 + part])
        for part in range(3)
    ]
    small = [
        pltpu.make_async_copy(source.at[row, pl.ds(size, 16)], rows.at[part], sems.at[6 + part])
        for part, (source, row) in enumerate(sources)
    ]
    for copy in inward + small:
        copy.start()
    for part in range(3):
        inward[part].wait()
        outward[part].start()
    for part in range(3):
        small[part].wait()
        values = rows[part, :, :units].astype(F32)
        bias[part] = values[0:1] + values[1:2] + values[2:3]
    for copy in outward:
        copy.wait()


def inner_rest(far, near):
    size = far.shape[1] - 16
    width = far.shape[2]
    held = pl.BlockSpec(memory_space=pltpu.HBM)
    return pl.pallas_call(
        collect_kernel,
        in_specs=[held, held],
        out_specs=[held, pl.BlockSpec(memory_space=pltpu.VMEM)],
        out_shape=[
            pltpu.HBM((1, 3, size, width), BF16),
            jax.ShapeDtypeStruct((3, 1, width // 2), F32),
        ],
        scratch_shapes=[
            pltpu.VMEM((3, size, width), BF16),
            pltpu.VMEM((3, 16, width), BF16),
            pltpu.SemaphoreType.DMA((9,)),
        ],
        cost_estimate=pl.CostEstimate(flops=0, bytes_accessed=12 * size * width, transcendentals=0),
        name="collect",
    )(far, near)


def inner_ids():
    quad, core = (lax.axis_index(name) for name in DATA)
    ids = []
    for flip in (0, 1):
        for quads in SQUARE_ORDER_INNER:
            for step in quads:
                ids.append((quad ^ step) * 2 + (core ^ flip))
    return jnp.stack(ids).astype(jnp.int32)


SQUARE_ORDER_INNER = ((0,), (1,), (2,), (3,))


def total_over_all(vectors, inner):
    width = vectors.shape[1]
    joined = jnp.concatenate([vectors, inner.reshape(-1, width)])
    joined = joined + swap(joined, "core", 1)
    along_x, along_y, across = (swap(joined, "quad", bit) for bit in (1, 2, 3))
    joined = (joined + along_x) + (along_y + across)
    count = vectors.shape[0]
    parts = [
        jnp.concatenate([joined[:count], joined[count + bit : count + bit + 1]]) for bit in range(4)
    ]
    own, near, far, last = [parts[0]] + [swap(parts[bit], "tp", bit) for bit in (1, 2, 3)]
    joined = (own + near) + (far + last)
    return joined[:count], joined[count:]


def shards(
    tokens,
    segment_ids,
    w_query,
    w_key,
    w_value,
    w_output,
    bias_query,
    bias_value,
    bias_output,
    gain_attn,
    beta_attn,
    w_inner,
    bias_inner,
    w_outer,
    bias_outer,
    gain_ffn,
    beta_ffn,
    cotangent,
):
    slots = segment_ids.shape[1]
    width = tokens.shape[1]
    line = lambda vector: vector.reshape(1, -1)
    quads, cores, layers = (lax.axis_size(name) for name in ALL)
    tuned = (quads, cores, layers) == (4, 2, 4)
    projections = jnp.stack([w_query, w_key, w_value])
    span = width // 2
    def attend_group(group, pieces, carried, token):
        first_column = group % 2 * (width // GROUPS)
        *carried, token = attend(
            tokens,
            seg_row,
            seg_col,
            pieces,
            block_ids,
            line(bias_query),
            line(bias_value),
            group,
            first_column,
            token,
            carried,
        )
        return carried, token

    def norm_of(mixed, pieces):
        return first_norm(tokens, mixed, pieces, block_ids, line(bias_output))

    def own_part(normal, own_in, own_bias, own_out):
        return own_inner(
            normal,
            line(gain_attn),
            line(beta_attn),
            line(bias_outer),
            own_in,
            line(own_bias),
            own_out,
        )

    token = jnp.zeros((8, 128), F32)
    seg_row = segment_ids.reshape(-1, 1, slots)
    seg_col = segment_ids.reshape(-1, 1)
    if tuned:
        own_in, own_out, own_bias = w_inner, w_outer, bias_inner
        block_ids = attention_ids()
        unit_ids = inner_ids()
        join = jnp.concatenate
        own = [projections[None, :, :, :span]]
        both = [w_output[:, i * span : (i + 1) * span] for i in range(2)]
        own.append(join([projections[:, :, span:], jnp.stack(both)])[None])
        units_own = inner_payloads(w_inner, bias_inner, w_outer)
        pair = join([own[0], swap(own[0], "tp", 2)])
        left = join([pair, swap(pair, "quad", 1)])
        next_far = swap(after(own[1], pair), "tp", 2)
        near = swap(pair, "tp", 1)
        near, seg_row, seg_col, block_ids, unit_ids, token = gate(
            near, seg_row, seg_col, block_ids, unit_ids, token
        )
        right = join([near, swap(near, "quad", 2)])
        next_pair = join([own[1], next_far])
        far = swap(after(units_own[0], next_far), "tp", 2)
        next_near = swap(after(next_pair, near), "tp", 1)
        first = [left, right, swap(left, "quad", 2), swap(right, "quad", 1)]
        bundle = with_sibling(first)
        next_left = join([next_pair, swap(next_pair, "quad", 1)])
        next_right = join([next_near, swap(next_near, "quad", 2)])
        unit_pair = join([units_own[0], far])
        token, next_left, next_right, unit_pair = gate(token, next_left, next_right, unit_pair)
        second = [
            next_left,
            next_right,
            swap(next_left, "quad", 2),
            swap(next_right, "quad", 1),
        ]
        unit_near = swap(unit_pair, "tp", 1)
        carried, token = attend_group(0, bundle, [], token)
        token, unit_near, *second = gate(token, unit_near, *second)
        rest, bias = inner_rest(far, unit_near)
        inner_bias = [bias]
        token, rest = gate(token, rest)
        around = [swap(rest, "quad", bit) for bit in (1, 2)]
        next_far = swap(after(units_own[1], unit_near), "tp", 2)
        carried, token = attend_group(1, bundle, carried, token)
        token, rest, next_far, *rest_of = gate(token, rest, next_far, *around, *second)
        around, second = rest_of[:2], rest_of[2:]
        next_bundle = with_sibling(second)
        next_far, rest, *next_bundle = gate(next_far, rest, *next_bundle)
        around.append(swap(rest, "quad", 3))
        next_near = swap(join([units_own[1], next_far]), "tp", 1)
        carried, token = attend_group(2, next_bundle, carried, token)
        token, next_near, rest, *around = gate(token, next_near, rest, *around)
        next_rest, bias = inner_rest(next_far, next_near)
        inner_bias.append(bias)
        token, next_rest = gate(token, next_rest)
        next_x, next_y = swap(next_rest, "quad", 1), swap(next_rest, "quad", 2)
        sibling = [swap(piece, "core", 1) for piece in (rest, *around[:2])]
        carried, token = attend_group(3, next_bundle, carried, token)
        carried[4], next_rest, around[2], *sibling = gate(
            carried[4], next_rest, around[2], *sibling
        )
        sibling.append(swap(around[2], "core", 1))
        inner = [[rest, *around, *sibling]]
        next_sibling = [swap(next_rest, "core", 1)]
        normal, scale, full_output = norm_of(carried[4], next_bundle)
        normal, next_x, next_y, *next_sibling = gate(normal, next_x, next_y, *next_sibling)
        half = next_rest.shape[2] // 2
        next_across = (
            swap(next_x[:, :, :half], "quad", 2),
            swap(next_y[:, :, half:], "quad", 1),
        )
        next_sibling += [swap(piece, "core", 1) for piece in (next_x, next_y)]
        outer, slope_own = own_part(normal, own_in, own_bias, own_out)
        outer, *rest_of = gate(outer, *next_across, *next_sibling)
        next_across, next_sibling = rest_of[:2], rest_of[2:]
        next_sibling += [swap(piece, "core", 1) for piece in next_across]
        inner.append([next_rest, next_x, next_y, *next_across, *next_sibling])
    else:
        full = lax.all_gather(projections, ALL, axis=1, tiled=True)
        more = lax.all_gather(w_output, ALL, axis=0, tiled=True)
        bundles = [
            jnp.concatenate(
                [full[:, :, i * span : (i + 1) * span], more[None, :, :span], more[None, :, span:]]
            )
            for i in range(2)
        ]
        bundles = [
            [bundle.reshape(5, BLOCKS, -1, span).transpose(1, 0, 2, 3)] for bundle in bundles
        ]
        block_ids = jnp.arange(BLOCKS, dtype=jnp.int32)
        units = width // 2
        full = lax.all_gather(w_inner, "tp", axis=1, tiled=True).reshape(8, 2, -1, 4, 2, units)
        own_in = full[:, :, :, 0].reshape(width, width)
        into = full[:, :, :, 1:].transpose(4, 0, 3, 2, 1, 5).reshape(2, 8, 3, -1, width)
        full = lax.all_gather(w_outer, "tp", axis=0, tiled=True).reshape(4, 2, 8, -1, width)
        own_out = full[0].reshape(width, width)
        out = full[1:].transpose(1, 2, 0, 3, 4)
        joined = jnp.concatenate([into, out], axis=3)
        inner = [[half[i : i + 1] for i in range(8)] for half in joined]
        full = lax.all_gather(bias_inner, "tp", axis=0, tiled=True).reshape(4, 1, width)
        own_bias, inner_bias = full[0, 0], [full[1:, :, :units], full[1:, :, units:]]
        unit_ids = jnp.arange(8, dtype=jnp.int32)
        carried = []
        for group in range(GROUPS):
            carried, token = attend_group(group, bundles[group // 2], carried, token)
        normal, scale, full_output = norm_of(carried[4], bundles[1])
        outer, slope_own = own_part(normal, own_in, own_bias, own_out)
    q, k, v, probs, mixed, full_projections = carried
    layer_out, first_grad, branch, sum_inner, sums = layer_step(
        normal,
        scale,
        outer,
        slope_own,
        cotangent,
        line(gain_attn),
        line(beta_attn),
        *inner_bias,
        line(gain_ffn),
        line(beta_ffn),
        own_in,
        own_out,
        inner,
        unit_ids,
    )
    tokens_grad, sum_q, sum_v = attend_backward(
        branch, first_grad, full_output, full_projections, q, k, v, mixed, probs, slots
    )
    vectors = jnp.concatenate([sum_q, sum_v, sums])
    if tuned:
        totals, inner_total = total_over_all(vectors, sum_inner)
        inner_total = inner_total[0]
    else:
        totals = lax.psum(vectors, ALL)
        inner_total = lax.psum(sum_inner.reshape(-1), ALL)
        units = w_inner.shape[1]
        inner_total = lax.dynamic_slice_in_dim(inner_total, lax.axis_index("tp") * units, units, 0)
    return (
        layer_out,
        tokens_grad,
        totals[0],
        totals[1],
        totals[2],
        totals[3],
        inner_total,
        totals[4],
        totals[5],
    )


def solution(mesh):
    dp, tp = mesh.shape["dp"], mesh.shape["tp"]
    split = Mesh(mesh.devices.reshape(dp // 2, 2, tp), ALL)
    spread = P(ALL, None)
    in_specs = (
        (spread,) * 6
        + (P(),) * 5
        + (P(None, "tp"), P("tp"), P("tp", None), P(), P(), P(), spread)
    )
    out_specs = (spread, spread, P(), P(), P(), P(), P("tp"), P(), P())
    return jax.shard_map(shards, mesh=split, in_specs=in_specs, out_specs=out_specs, check_vma=False)
```

```python
import functools
import math

import jax
import jax.numpy as jnp
from jax import lax
from jax.experimental import pallas as pl
from jax.experimental.pallas import tpu as pltpu
from jax.sharding import Mesh
from jax.sharding import PartitionSpec as P

HEADS = 16
F32 = jnp.float32
BF16 = jnp.bfloat16
NORM_EPSILON = 1e-12
LOG2E = math.log2(math.e)
LN2 = math.log(2.0)
MIB = 2**20
VMEM = 60 * MIB
keep = pltpu.HBM
spill = pltpu.HBM


def dot(left, right):
    return jnp.dot(left, right, preferred_element_type=F32)


def dot_nt(left, right):
    return lax.dot_general(left, right, (((1,), (1,)), ((), ())), preferred_element_type=F32)


def column_sum(values):
    return jnp.sum(values.astype(F32), axis=0, keepdims=True)


def normalize(resid):
    centered = resid - jnp.mean(resid, axis=-1, keepdims=True)
    spread = jnp.mean(centered * centered, axis=-1, keepdims=True)
    scale = lax.rsqrt(spread + NORM_EPSILON)
    return centered * scale, scale


def norm_back(grad, gain, normal, scale):
    weighted = grad * gain
    return scale * (
        weighted
        - jnp.mean(weighted, axis=-1, keepdims=True)
        - normal * jnp.mean(weighted * normal, axis=-1, keepdims=True)
    )


def gelu_parts(value):
    size = jnp.abs(value)
    step = 1.0 / (1.0 + (0.3275911 / math.sqrt(2.0)) * size)
    bell = jnp.exp2(value * value * (-0.5 * LOG2E))
    series = step * (
        0.5 * 0.254829592
        + step
        * (
            0.5 * -0.284496736
            + step * (0.5 * 1.421413741 + step * (0.5 * -1.453152027 + step * (0.5 * 1.061405429)))
        )
    )
    tail = series * bell
    share = jnp.where(value >= 0, 1.0 - tail, tail)
    return value * share, share + value * bell * (1.0 / math.sqrt(2.0 * math.pi))


def block_copies(ids, pieces, first, column, target, sems):
    copies = []
    for piece in pieces:
        for block in range(piece.shape[0]):
            number = len(copies)
            height = piece.shape[2]
            start = pl.multiple_of(ids[number] * height, height)
            copies.append(
                pltpu.make_async_copy(
                    piece.at[
                        block, pl.ds(first, target.shape[0]), :, pl.ds(column, target.shape[2])
                    ],
                    target.at[:, pl.ds(start, height), :],
                    sems.at[number],
                )
            )
    return copies


def unit_copies(ids, pieces, part, first_unit, w_in, w_out, sems):
    copies = []
    per = len(pieces) // 2
    for number, piece in enumerate(pieces):
        flip, kind = divmod(number, per)
        place = ids[flip * 4 + min(kind, 3)]
        split = per == 5 and kind >= 3
        height = piece.shape[2] if split else piece.shape[2] // 2
        half = piece.shape[3] // 2
        columns = pl.ds(first_unit, half)
        if not split or kind == 3:
            top = pl.ds(0, height)
            for lower in range(2):
                start = pl.multiple_of(place * (2 * height) + lower * height, height)
                copies.append(
                    pltpu.make_async_copy(
                        piece.at[0, part, top, pl.ds(lower * half, half)],
                        w_in.at[pl.ds(start, height), columns],
                        sems.at[0],
                    )
                )
        if not split or kind == 4:
            start = pl.multiple_of(place * height + first_unit, height)
            copies.append(
                pltpu.make_async_copy(
                    piece.at[0, part, pl.ds(0 if split else height, height), :],
                    w_out.at[pl.ds(start, height), :],
                    sems.at[1],
                )
            )
    return copies


def attend_kernel(head_size, first_column, count_pieces, carried, ids, *refs):
    seg_row, seg_col, x, bq, bv = refs[:5]
    pieces = refs[6 : 6 + count_pieces]
    refs = refs[6 + count_pieces + carried :]
    q_out, k_out, v_out, probs_out, mixed_out, weights, token, sems = refs
    group = q_out.shape[1] // head_size
    factor = head_size ** (-0.5) * LOG2E

    @pl.when(pl.program_id(0) == 0)
    def _():
        token[...] = jnp.zeros_like(token)
        copies = block_copies(ids, pieces, 0, first_column, weights, sems)
        for copy in copies:
            copy.start()
        for copy in copies:
            copy.wait()

    q_out[...] = ((dot(x[...], weights[0]) + bq[...]) * factor).astype(BF16)
    k_out[...] = dot(x[...], weights[1]).astype(BF16)
    v_out[...] = (dot(x[...], weights[2]) + bv[...]).astype(BF16)
    same_doc = seg_col[...] == seg_row[0]
    parts = []
    lanes_of = lambda head: slice(head * head_size, (head + 1) * head_size)
    every = [dot_nt(k_out[:, lanes_of(head)], q_out[:, lanes_of(head)]) for head in range(group)]
    for head in range(group):
        scores = jnp.where(same_doc, every[head], -1000000000.0)
        top = jnp.max(scores, axis=0, keepdims=True)
        powers = jnp.exp2(scores - top)
        total = jnp.sum(powers, axis=0, keepdims=True)
        probs = (powers * (1.0 / total)).astype(BF16)
        probs_out[0, 0, head] = probs
        parts.append(dot(v_out[:, lanes_of(head)].T, probs))
    mixed_out[...] = jnp.concatenate(parts, axis=0).T.astype(BF16)


GROUPS = 4


def attend(tokens, seg_row, seg_col, pieces, ids, bq, bv, group, first_column, token, carried):
    count, width = tokens.shape
    rows, _, slots = seg_row.shape
    head_size = width // HEADS
    lanes = width // GROUPS
    heads = HEADS // GROUPS
    block = lambda cols, at: pl.BlockSpec((slots, cols), lambda r, ids: (r, at))
    line = pl.BlockSpec((1, lanes), lambda r, ids: (0, group))
    anywhere = pl.BlockSpec(memory_space=pltpu.HBM)
    shaped = jax.ShapeDtypeStruct
    blocks = sum(piece.shape[0] for piece in pieces)
    return pl.pallas_call(
        functools.partial(attend_kernel, head_size, first_column, len(pieces), len(carried)),
        grid_spec=pltpu.PrefetchScalarGridSpec(
            num_scalar_prefetch=1,
            grid=(rows,),
            in_specs=[
                pl.BlockSpec((1, 1, slots), lambda r, ids: (r, 0, 0)),
                block(1, 0),
                block(width, 0),
                line,
                line,
            ]
            + [anywhere] * (1 + len(pieces) + len(carried)),
            out_specs=[
                block(lanes, group),
                block(lanes, group),
                block(lanes, group),
                pl.BlockSpec((1, 1, heads, slots, slots), lambda r, ids: (group, r, 0, 0, 0)),
                block(lanes, group),
                pl.BlockSpec((3, width, lanes), lambda r, ids: (0, 0, group)),
                pl.BlockSpec((8, 128), lambda r, ids: (0, 0)),
            ],
            scratch_shapes=[pltpu.SemaphoreType.DMA((blocks,))],
        ),
        out_shape=[
            spill((count, width), BF16),
            spill((count, width), BF16),
            spill((count, width), BF16),
            spill((GROUPS, rows, heads, slots, slots), BF16),
            spill((count, width), BF16),
            spill((3, width, width), BF16),
            shaped((8, 128), F32),
        ],
        input_output_aliases={7 + len(pieces) + i: i for i in range(len(carried))},
        compiler_params=pltpu.CompilerParams(vmem_limit_bytes=VMEM),
        cost_estimate=pl.CostEstimate(
            flops=(6 * count * width * width + 16 * count * slots * width) // GROUPS,
            bytes_accessed=40 * 2**20 // GROUPS,
            transcendentals=count * slots * HEADS // GROUPS,
        ),
        name="attend",
    )(
        ids,
        seg_row,
        seg_col,
        tokens,
        bq,
        bv,
        token,
        *pieces,
        *carried,
    )


TILE = 512


def first_norm_kernel(count_pieces, ids, x, mixed, bo, *refs):
    pieces = refs[:count_pieces]
    normal_out, scale_out, wo_out, wo, sems = refs[count_pieces:]

    @pl.when(pl.program_id(0) == 0)
    def _():
        copies = block_copies(ids, pieces, 3, 0, wo, sems)
        for copy in copies:
            copy.start()
        for copy in copies:
            copy.wait()
        half = wo.shape[2]
        wo_out[:, :half] = wo[0]
        wo_out[:, half:] = wo[1]

    resid = x[...].astype(F32) + dot(mixed[...], wo_out[...]) + bo[...]
    normal_out[...], scale_out[...] = normalize(resid)


def first_norm(tokens, mixed, pieces, ids, bo):
    count, width = tokens.shape
    tile = 256
    whole = lambda shape: pl.BlockSpec(shape, lambda i, ids: (0,) * len(shape))
    rows = lambda cols: pl.BlockSpec((tile, cols), lambda i, ids: (i, 0))
    held = pl.BlockSpec(memory_space=pltpu.HBM)
    blocks = sum(piece.shape[0] for piece in pieces)
    return pl.pallas_call(
        functools.partial(first_norm_kernel, len(pieces)),
        grid_spec=pltpu.PrefetchScalarGridSpec(
            num_scalar_prefetch=1,
            grid=(count // tile,),
            in_specs=[rows(width), rows(width), whole((1, width))] + [held] * len(pieces),
            out_specs=[rows(width), rows(1), whole((width, width))],
            scratch_shapes=[
                pltpu.VMEM((2, width, width // 2), BF16),
                pltpu.SemaphoreType.DMA((blocks,)),
            ],
        ),
        out_shape=[
            spill((count, width), F32),
            spill((count, 1), F32),
            spill((width, width), BF16),
        ],
        compiler_params=pltpu.CompilerParams(vmem_limit_bytes=VMEM),
        cost_estimate=pl.CostEstimate(
            flops=8 * count * width * width, bytes_accessed=16 * 2**20, transcendentals=0
        ),
        name="first_norm",
    )(ids, tokens, mixed, bo, *pieces)


def own_inner_kernel(normal, gain, beta, b_outer, w_in, b_in, w_out, total, slope_out):
    hidden = normal[...] * gain[...] + beta[...]
    act, slope = gelu_parts(dot(hidden.astype(BF16), w_in[...]) + b_in[...])
    slope_out[...] = slope.astype(BF16)
    total[...] = hidden + b_outer[...] + dot(act.astype(BF16), w_out[...])


def own_inner(normal, gain, beta, b_outer, w_in, b_in, w_out):
    count, width = normal.shape
    units = w_in.shape[1]
    tile = 256
    whole = lambda shape: pl.BlockSpec(shape, lambda i: (0,) * len(shape))
    rows = lambda cols: pl.BlockSpec((tile, cols), lambda i: (i, 0))
    vector = whole((1, width))
    return pl.pallas_call(
        own_inner_kernel,
        grid=(count // tile,),
        in_specs=[
            rows(width),
            vector,
            vector,
            vector,
            whole((width, units)),
            whole((1, units)),
            whole((units, width)),
        ],
        out_specs=[rows(width), rows(units)],
        out_shape=[spill((count, width), F32), spill((count, units), BF16)],
        compiler_params=pltpu.CompilerParams(vmem_limit_bytes=VMEM),
        cost_estimate=pl.CostEstimate(
            flops=8 * count * width * units, bytes_accessed=14 * 2**20, transcendentals=0
        ),
        name="own_inner",
    )(normal, gain, beta, b_outer, w_in, b_in, w_out)


def layer_kernel(
    counts,
    ids,
    normal,
    scale,
    before,
    slope_own,
    cot,
    gain_attn,
    beta_attn,
    b_even,
    b_odd,
    gain_ffn,
    beta_ffn,
    *refs,
):
    own_in_ref, own_out_ref = refs[:2]
    refs = refs[2:]
    bundles = []
    for count in counts:
        bundles.append(refs[:count])
        refs = refs[count:]
    (
        layer_out,
        first_grad,
        branch_grad,
        sum_inner,
        sums,
        w_in,
        w_out,
        slopes,
        even,
        odd,
        total,
        low,
        sems,
    ) = refs
    first = pl.program_id(0) == 0
    chunks, _, units = w_in.shape

    def chunk_copies(chunk):
        if chunk == 0:
            return [
                pltpu.make_async_copy(own_in_ref, w_in.at[0], sems.at[0, 0]),
                pltpu.make_async_copy(own_out_ref, w_out.at[0], sems.at[0, 1]),
            ]
        copies = []
        for number in range(2):
            copies += unit_copies(
                ids,
                bundles[number],
                chunk - 1,
                number * (units // 2),
                w_in.at[chunk],
                w_out.at[chunk],
                sems.at[chunk],
            )
        return copies

    def arrived(chunk, which, target):
        @pl.when(first)
        def _():
            whole = target.at[chunk]
            pltpu.make_async_copy(whole, whole, sems.at[chunk, which]).wait()

    @pl.when(first)
    def _():
        for chunk in (*range(1, chunks), 0):
            for copy in chunk_copies(chunk):
                copy.start()
        sums[...] = jnp.zeros_like(sums)
        sum_inner[...] = jnp.zeros_like(sum_inner)

    low[...] = (normal[...] * gain_attn[...] + beta_attn[...]).astype(BF16)
    total[...] = before[...]
    slopes[0] = slope_own[...]
    buffers = (even, odd)
    arrived(1, 0, w_in)
    biases = [jnp.concatenate([b_even[i], b_odd[i]], axis=1) for i in range(chunks - 1)]
    even[...] = dot(low[...], w_in[1]) + biases[0]
    for chunk in range(1, chunks):
        source, target = buffers[(chunk - 1) % 2], buffers[chunk % 2]
        arrived(chunk, 1, w_out)
        if chunk + 1 < chunks:
            arrived(chunk + 1, 0, w_in)
            target[...] = dot(low[...], w_in[chunk + 1]) + biases[chunk]
        act, slope = gelu_parts(source[...])
        slopes[chunk] = slope.astype(BF16)
        total[...] += dot(act.astype(BF16), w_out[chunk])
    arrived(0, 0, w_in)
    arrived(0, 1, w_out)

    unit, scale_two = normalize(total[...])
    layer_out[...] = (unit * gain_ffn[...] + beta_ffn[...]).astype(BF16)
    grad = cot[...].astype(F32)
    second = norm_back(grad, gain_ffn[...], unit, scale_two)
    low[...] = second.astype(BF16)
    sums[3:4, :] += column_sum(grad)
    sums[2:3, :] += column_sum(low[...])
    total[...] = second
    even[...] = dot_nt(low[...], w_out[0])

    def back(pair, step, source, target):
        chunk = 2 * pair + step
        target[...] = dot_nt(low[...], w_out[lax.rem(chunk + 1, chunks)])
        inner_grad = (slopes[chunk].astype(F32) * source[...]).astype(BF16)
        sum_inner[chunk] += column_sum(inner_grad)
        total[...] += dot_nt(inner_grad, w_in[chunk])

    @pl.loop(0, chunks // 2)
    def _(pair):
        back(pair, 0, even, odd)
        back(pair, 1, odd, even)

    sums[1:2, :] += column_sum(total[...])
    grad = norm_back(total[...], gain_attn[...], normal[...], scale[...])
    first_grad[...] = grad
    branch = grad.astype(BF16)
    branch_grad[...] = branch
    sums[0:1, :] += column_sum(branch)


def layer_step(
    normal,
    scale,
    before,
    slope_own,
    cot,
    gain_attn,
    beta_attn,
    b_even,
    b_odd,
    gain_ffn,
    beta_ffn,
    own_in,
    own_out,
    bundles,
    ids,
):
    count, width = normal.shape
    chunks = b_even.shape[0] + 1
    units = 2 * b_even.shape[2]
    whole = lambda shape: pl.BlockSpec(shape, lambda i, ids: (0,) * len(shape))
    rows = lambda cols: pl.BlockSpec((TILE, cols), lambda i, ids: (i, 0))
    vector = whole((1, width))
    held = pl.BlockSpec(memory_space=pltpu.HBM)
    shaped = jax.ShapeDtypeStruct
    return pl.pallas_call(
        functools.partial(layer_kernel, [len(group) for group in bundles]),
        grid_spec=pltpu.PrefetchScalarGridSpec(
            num_scalar_prefetch=1,
            grid=(count // TILE,),
            in_specs=[
                rows(width),
                rows(1),
                rows(width),
                rows(units),
                rows(width),
                vector,
                vector,
                whole(b_even.shape),
                whole(b_odd.shape),
                vector,
                vector,
            ]
            + [held] * (2 + sum(len(group) for group in bundles)),
            out_specs=[
                rows(width),
                rows(width),
                rows(width),
                whole((chunks, 1, units)),
                whole((4, width)),
            ],
            scratch_shapes=[
                pltpu.VMEM((chunks, width, units), BF16),
                pltpu.VMEM((chunks, units, width), BF16),
                pltpu.VMEM((chunks, TILE, units), BF16),
                pltpu.VMEM((TILE, units), F32),
                pltpu.VMEM((TILE, units), F32),
                pltpu.VMEM((TILE, width), F32),
                pltpu.VMEM((TILE, width), BF16),
                pltpu.SemaphoreType.DMA((chunks, 2)),
            ],
        ),
        out_shape=[
            spill((count, width), BF16),
            spill((count, width), F32),
            spill((count, width), BF16),
            shaped((chunks, 1, units), F32),
            shaped((4, width), F32),
        ],
        compiler_params=pltpu.CompilerParams(vmem_limit_bytes=VMEM),
        cost_estimate=pl.CostEstimate(
            flops=2 * count * width * (4 * units * chunks),
            bytes_accessed=36 * 2**20,
            transcendentals=0,
        ),
        name="layer_step",
    )(
        ids,
        normal,
        scale,
        before,
        slope_own,
        cot,
        gain_attn,
        beta_attn,
        b_even,
        b_odd,
        gain_ffn,
        beta_ffn,
        own_in,
        own_out,
        *bundles[0],
        *bundles[1],
    )


def attend_back_kernel(
    head_size, slots, branch, first, wo, weights, q, k, v, mixed, probs_in, out, sum_q, sum_v, grads,
    low_grad, product
):
    count = branch.shape[0]
    width = wo.shape[0]
    group = width // head_size
    low_grad[...] = dot_nt(branch[...], wo[...]).astype(BF16)
    product[...] = low_grad[...].astype(F32) * mixed[...].astype(F32)

    @pl.loop(0, count // slots)
    def _(row):
        span = pl.ds(pl.multiple_of(row * slots, slots), slots)
        turned = product[span, :].T
        keys_turned = k[span, :].T
        queries_turned = q[span, :].T
        grad_turned = low_grad[span, :].T
        queries_grad = []
        keys_grad = []
        values_grad = []
        for head in range(group):
            lanes = slice(head * head_size, (head + 1) * head_size)
            probs = probs_in[0, row, head]
            shift = jnp.sum(turned[lanes, :], axis=0, keepdims=True)
            reach = dot_nt(v[span, lanes], low_grad[span, lanes])
            score_grad = (probs.astype(F32) * (reach - shift)).astype(BF16)
            values_grad.append(dot_nt(grad_turned[lanes, :], probs))
            keys_grad.append(dot_nt(queries_turned[lanes, :], score_grad))
            queries_grad.append(dot(keys_turned[lanes, :], score_grad))
        for place, (parts, factor) in enumerate(
            ((queries_grad, head_size ** (-0.5)), (keys_grad, LN2), (values_grad, 1.0))
        ):
            turned_back = jnp.concatenate(parts, axis=0).T * factor
            grads[span, place * width : (place + 1) * width] = turned_back.astype(BF16)
    sum_q[...] = column_sum(grads[:, :width])
    sum_v[...] = column_sum(grads[:, 2 * width :])
    joined = jnp.concatenate([weights[0], weights[1], weights[2]], axis=1)
    start = pl.program_id(0) == 0

    @pl.when(start)
    def _():
        for row in range(0, count, slots):
            span = slice(row, row + slots)
            out[span, :] = first[span, :] + dot_nt(grads[span, :], joined)

    @pl.when(jnp.logical_not(start))
    def _():
        for row in range(0, count, slots):
            span = slice(row, row + slots)
            out[span, :] += dot_nt(grads[span, :], joined)


def attend_backward(branch, first, wo, weights, q, k, v, mixed, probs, slots):
    count, width = branch.shape
    groups, rows, heads = probs.shape[:3]
    lanes = width // groups
    column = lambda height: pl.BlockSpec((height, lanes), lambda g: (0, g))
    whole = pl.BlockSpec((count, width), lambda g: (0, 0), pipeline_mode=pl.Buffered(1))
    shaped = jax.ShapeDtypeStruct
    return pl.pallas_call(
        functools.partial(attend_back_kernel, width // HEADS, slots),
        grid=(groups,),
        in_specs=[
            whole,
            whole,
            pl.BlockSpec((lanes, width), lambda g: (g, 0)),
            pl.BlockSpec((3, width, lanes), lambda g: (0, 0, g)),
            column(count),
            column(count),
            column(count),
            column(count),
            pl.BlockSpec((1, rows, heads, slots, slots), lambda g: (g, 0, 0, 0, 0)),
        ],
        out_specs=[pl.BlockSpec((count, width), lambda g: (0, 0)), column(1), column(1)],
        out_shape=[
            spill((count, width), F32),
            shaped((1, width), F32),
            shaped((1, width), F32),
        ],
        scratch_shapes=[
            pltpu.VMEM((count, 3 * lanes), BF16),
            pltpu.VMEM((count, lanes), BF16),
            pltpu.VMEM((count, lanes), F32),
        ],
        compiler_params=pltpu.CompilerParams(vmem_limit_bytes=VMEM),
        cost_estimate=pl.CostEstimate(
            flops=8 * count * width * width + 32 * count * slots * width,
            bytes_accessed=44 * 2**20,
            transcendentals=0,
        ),
        name="attend_backward",
    )(branch, first, wo, weights, q, k, v, mixed, probs)


ALL = ("quad", "core", "tp")
DATA = ("quad", "core")
BLOCKS = 32


def swap(value, axis, bit):
    size = lax.axis_size(axis)
    return lax.ppermute(value, axis, [(i, i ^ bit) for i in range(size)])


def after(value, token):
    return lax.optimization_barrier((value, token))[0]


def gate(*values):
    return lax.optimization_barrier(values)


def with_sibling(pieces):
    return list(pieces) + [swap(piece, "core", 1) for piece in pieces]


SQUARE_ORDER = ((0, 1), (0, 2), (2, 3), (1, 3))


def attention_ids():
    quad, core, layer = (lax.axis_index(name) for name in ALL)
    ids = []
    for flip in (0, 1):
        for quads, layers in zip(SQUARE_ORDER, ((0, 2), (1, 3), (0, 2), (1, 3))):
            for step in quads:
                for far in layers:
                    ids.append((((quad ^ step) * 2 + (core ^ flip)) * 4) + (layer ^ far))
    return jnp.stack(ids).astype(jnp.int32)


def inner_payloads(w_inner, bias_inner, w_outer):
    place = lax.axis_index(DATA)
    units = w_inner.shape[1] // 2
    high = bias_inner.astype(BF16)
    rest = bias_inner - high.astype(F32)
    middle = rest.astype(BF16)
    low = (rest - middle.astype(F32)).astype(BF16)
    step = w_inner.shape[0] // 16
    payloads = []
    for bundle in range(2):
        span = slice(bundle * units, (bundle + 1) * units)
        rows = lax.dynamic_slice_in_dim(w_inner, place * 2 * step, 2 * step, 0)[:, span]
        payload = [
            rows[:step],
            rows[step:],
        ]
        payload = jnp.concatenate(payload, axis=1)
        more = lax.dynamic_slice_in_dim(w_outer, bundle * units + place * step, step, 0)
        bias = jnp.concatenate([part[span].reshape(1, units) for part in (high, middle, low)])
        bias = jnp.pad(bias, ((0, 13), (0, units)))
        payloads.append(jnp.concatenate([payload, more, bias])[None])
    return payloads


def collect_kernel(far, near, rest, bias, held, rows, sems):
    size = rest.shape[2]
    units = bias.shape[2]
    sources = ((near, 0), (far, 0), (near, 1))
    inward = [
        pltpu.make_async_copy(source.at[row, pl.ds(0, size)], held.at[part], sems.at[part])
        for part, (source, row) in enumerate(sources)
    ]
    outward = [
        pltpu.make_async_copy(held.at[part], rest.at[0, part], sems.at[3 + part])
        for part in range(3)
    ]
    small = [
        pltpu.make_async_copy(source.at[row, pl.ds(size, 16)], rows.at[part], sems.at[6 + part])
        for part, (source, row) in enumerate(sources)
    ]
    for copy in inward + small:
        copy.start()
    for part in range(3):
        inward[part].wait()
        outward[part].start()
    for part in range(3):
        small[part].wait()
        values = rows[part, :, :units].astype(F32)
        bias[part] = values[0:1] + values[1:2] + values[2:3]
    for copy in outward:
        copy.wait()


def inner_rest(far, near):
    size = far.shape[1] - 16
    width = far.shape[2]
    held = pl.BlockSpec(memory_space=pltpu.HBM)
    return pl.pallas_call(
        collect_kernel,
        in_specs=[held, held],
        out_specs=[held, pl.BlockSpec(memory_space=pltpu.VMEM)],
        out_shape=[
            pltpu.HBM((1, 3, size, width), BF16),
            jax.ShapeDtypeStruct((3, 1, width // 2), F32),
        ],
        scratch_shapes=[
            pltpu.VMEM((3, size, width), BF16),
            pltpu.VMEM((3, 16, width), BF16),
            pltpu.SemaphoreType.DMA((9,)),
        ],
        cost_estimate=pl.CostEstimate(flops=0, bytes_accessed=12 * size * width, transcendentals=0),
        name="collect",
    )(far, near)


def inner_ids():
    quad, core = (lax.axis_index(name) for name in DATA)
    ids = []
    for flip in (0, 1):
        for quads in SQUARE_ORDER_INNER:
            for step in quads:
                ids.append((quad ^ step) * 2 + (core ^ flip))
    return jnp.stack(ids).astype(jnp.int32)


SQUARE_ORDER_INNER = ((0,), (1,), (2,), (3,))


def total_over_all(vectors, inner):
    width = vectors.shape[1]
    joined = jnp.concatenate([vectors, inner.reshape(-1, width)])
    joined = joined + swap(joined, "core", 1)
    along_x, along_y, across = (swap(joined, "quad", bit) for bit in (1, 2, 3))
    joined = (joined + along_x) + (along_y + across)
    count = vectors.shape[0]
    parts = [
        jnp.concatenate([joined[:count], joined[count + bit : count + bit + 1]]) for bit in range(4)
    ]
    own, near, far, last = [parts[0]] + [swap(parts[bit], "tp", bit) for bit in (1, 2, 3)]
    joined = (own + near) + (far + last)
    return joined[:count], joined[count:]


def shards(
    tokens,
    segment_ids,
    w_query,
    w_key,
    w_value,
    w_output,
    bias_query,
    bias_value,
    bias_output,
    gain_attn,
    beta_attn,
    w_inner,
    bias_inner,
    w_outer,
    bias_outer,
    gain_ffn,
    beta_ffn,
    cotangent,
):
    slots = segment_ids.shape[1]
    width = tokens.shape[1]
    line = lambda vector: vector.reshape(1, -1)
    quads, cores, layers = (lax.axis_size(name) for name in ALL)
    tuned = (quads, cores, layers) == (4, 2, 4)
    projections = jnp.stack([w_query, w_key, w_value])
    span = width // 2
    def attend_group(group, pieces, carried, token):
        first_column = group % 2 * (width // GROUPS)
        *carried, token = attend(
            tokens,
            seg_row,
            seg_col,
            pieces,
            block_ids,
            line(bias_query),
            line(bias_value),
            group,
            first_column,
            token,
            carried,
        )
        return carried, token

    def norm_of(mixed, pieces):
        return first_norm(tokens, mixed, pieces, block_ids, line(bias_output))

    def own_part(normal, own_in, own_bias, own_out):
        return own_inner(
            normal,
            line(gain_attn),
            line(beta_attn),
            line(bias_outer),
            own_in,
            line(own_bias),
            own_out,
        )

    token = jnp.zeros((8, 128), F32)
    seg_row = segment_ids.reshape(-1, 1, slots)
    seg_col = segment_ids.reshape(-1, 1)
    if tuned:
        own_in, own_out, own_bias = w_inner, w_outer, bias_inner
        block_ids = attention_ids()
        unit_ids = inner_ids()
        join = jnp.concatenate
        own = [projections[None, :, :, :span]]
        both = [w_output[:, i * span : (i + 1) * span] for i in range(2)]
        own.append(join([projections[:, :, span:], jnp.stack(both)])[None])
        units_own = inner_payloads(w_inner, bias_inner, w_outer)
        pair = join([own[0], swap(own[0], "tp", 2)])
        left = join([pair, swap(pair, "quad", 1)])
        next_far = swap(after(own[1], pair), "tp", 2)
        near = swap(pair, "tp", 1)
        near, seg_row, seg_col, block_ids, unit_ids, token = gate(
            near, seg_row, seg_col, block_ids, unit_ids, token
        )
        right = join([near, swap(near, "quad", 2)])
        next_pair = join([own[1], next_far])
        far = swap(after(units_own[0], next_far), "tp", 2)
        next_near = swap(after(next_pair, near), "tp", 1)
        first = [left, right, swap(left, "quad", 2), swap(right, "quad", 1)]
        bundle = with_sibling(first)
        next_left = join([next_pair, swap(next_pair, "quad", 1)])
        next_right = join([next_near, swap(next_near, "quad", 2)])
        unit_pair = join([units_own[0], far])
        token, next_left, next_right, unit_pair = gate(token, next_left, next_right, unit_pair)
        second = [
            next_left,
            next_right,
            swap(next_left, "quad", 2),
            swap(next_right, "quad", 1),
        ]
        unit_near = swap(unit_pair, "tp", 1)
        carried, token = attend_group(0, bundle, [], token)
        token, unit_near, *second = gate(token, unit_near, *second)
        rest, bias = inner_rest(far, unit_near)
        inner_bias = [bias]
        token, rest = gate(token, rest)
        around = [swap(rest, "quad", bit) for bit in (1, 2)]
        next_far = swap(after(units_own[1], unit_near), "tp", 2)
        carried, token = attend_group(1, bundle, carried, token)
        token, rest, next_far, *rest_of = gate(token, rest, next_far, *around, *second)
        around, second = rest_of[:2], rest_of[2:]
        next_bundle = with_sibling(second)
        next_far, rest, *next_bundle = gate(next_far, rest, *next_bundle)
        around.append(swap(rest, "quad", 3))
        next_near = swap(join([units_own[1], next_far]), "tp", 1)
        carried, token = attend_group(2, next_bundle, carried, token)
        token, next_near, rest, *around = gate(token, next_near, rest, *around)
        next_rest, bias = inner_rest(next_far, next_near)
        inner_bias.append(bias)
        token, next_rest = gate(token, next_rest)
        next_x, next_y = swap(next_rest, "quad", 1), swap(next_rest, "quad", 2)
        sibling = [swap(piece, "core", 1) for piece in (rest, *around[:2])]
        carried, token = attend_group(3, next_bundle, carried, token)
        carried[4], next_rest, around[2], *sibling = gate(
            carried[4], next_rest, around[2], *sibling
        )
        sibling.append(swap(around[2], "core", 1))
        inner = [[rest, *around, *sibling]]
        next_sibling = [swap(next_rest, "core", 1)]
        normal, scale, full_output = norm_of(carried[4], next_bundle)
        normal, next_x, next_y, *next_sibling = gate(normal, next_x, next_y, *next_sibling)
        half = next_rest.shape[2] // 2
        next_across = (
            swap(next_x[:, :, :half], "quad", 2),
            swap(next_y[:, :, half:], "quad", 1),
        )
        next_sibling += [swap(piece, "core", 1) for piece in (next_x, next_y)]
        outer, slope_own = own_part(normal, own_in, own_bias, own_out)
        outer, *rest_of = gate(outer, *next_across, *next_sibling)
        next_across, next_sibling = rest_of[:2], rest_of[2:]
        next_sibling += [swap(piece, "core", 1) for piece in next_across]
        inner.append([next_rest, next_x, next_y, *next_across, *next_sibling])
    else:
        full = lax.all_gather(projections, ALL, axis=1, tiled=True)
        more = lax.all_gather(w_output, ALL, axis=0, tiled=True)
        bundles = [
            jnp.concatenate(
                [full[:, :, i * span : (i + 1) * span], more[None, :, :span], more[None, :, span:]]
            )
            for i in range(2)
        ]
        bundles = [
            [bundle.reshape(5, BLOCKS, -1, span).transpose(1, 0, 2, 3)] for bundle in bundles
        ]
        block_ids = jnp.arange(BLOCKS, dtype=jnp.int32)
        units = width // 2
        full = lax.all_gather(w_inner, "tp", axis=1, tiled=True).reshape(8, 2, -1, 4, 2, units)
        own_in = full[:, :, :, 0].reshape(width, width)
        into = full[:, :, :, 1:].transpose(4, 0, 3, 2, 1, 5).reshape(2, 8, 3, -1, width)
        full = lax.all_gather(w_outer, "tp", axis=0, tiled=True).reshape(4, 2, 8, -1, width)
        own_out = full[0].reshape(width, width)
        out = full[1:].transpose(1, 2, 0, 3, 4)
        joined = jnp.concatenate([into, out], axis=3)
        inner = [[half[i : i + 1] for i in range(8)] for half in joined]
        full = lax.all_gather(bias_inner, "tp", axis=0, tiled=True).reshape(4, 1, width)
        own_bias, inner_bias = full[0, 0], [full[1:, :, :units], full[1:, :, units:]]
        unit_ids = jnp.arange(8, dtype=jnp.int32)
        carried = []
        for group in range(GROUPS):
            carried, token = attend_group(group, bundles[group // 2], carried, token)
        normal, scale, full_output = norm_of(carried[4], bundles[1])
        outer, slope_own = own_part(normal, own_in, own_bias, own_out)
    q, k, v, probs, mixed, full_projections = carried
    layer_out, first_grad, branch, sum_inner, sums = layer_step(
        normal,
        scale,
        outer,
        slope_own,
        cotangent,
        line(gain_attn),
        line(beta_attn),
        *inner_bias,
        line(gain_ffn),
        line(beta_ffn),
        own_in,
        own_out,
        inner,
        unit_ids,
    )
    tokens_grad, sum_q, sum_v = attend_backward(
        branch, first_grad, full_output, full_projections, q, k, v, mixed, probs, slots
    )
    vectors = jnp.concatenate([sum_q, sum_v, sums])
    if tuned:
        totals, inner_total = total_over_all(vectors, sum_inner)
        inner_total = inner_total[0]
    else:
        totals = lax.psum(vectors, ALL)
        inner_total = lax.psum(sum_inner.reshape(-1), ALL)
        units = w_inner.shape[1]
        inner_total = lax.dynamic_slice_in_dim(inner_total, lax.axis_index("tp") * units, units, 0)
    return (
        layer_out,
        tokens_grad,
        totals[0],
        totals[1],
        totals[2],
        totals[3],
        inner_total,
        totals[4],
        totals[5],
    )


def solution(mesh):
    dp, tp = mesh.shape["dp"], mesh.shape["tp"]
    split = Mesh(mesh.devices.reshape(dp // 2, 2, tp), ALL)
    spread = P(ALL, None)
    in_specs = (
        (spread,) * 6
        + (P(),) * 5
        + (P(None, "tp"), P("tp"), P("tp", None), P(), P(), P(), spread)
    )
    out_specs = (spread, spread, P(), P(), P(), P(), P("tp"), P(), P())
    return jax.shard_map(shards, mesh=split, in_specs=in_specs, out_specs=out_specs, check_vma=False)
```
